32 devices in a mesh: dp: 16 (over z, x, core), tensor: 2 (over y).
Axes of the slice: x: 2, y: 2, z: 4, core: 2. Of those that a mesh axis runs over, the one named last changes fastest.
Arguments:
- block_input: bfloat16 [32, 192, 2560], P(None, 'dp'), may hold values from -6 to 6
- cotangent: bfloat16 [32, 192, 2560], P(None, 'dp'), may hold values from -6 to 6
- seq_lengths: int32 [32], replicated, may hold values from 1 to 192, 4608 in all
- pre_gain: bfloat16 [2560], P('dp'), may hold values from -0.5 to 0.5
- w_branch: bfloat16 [2560, 2560], P('dp', 'tensor'), may hold values from -0.125 to 0.125
- b_branch: bfloat16 [10, 256], P('tensor', 'dp'), may hold values from -3 to 3
- w_recur: bfloat16 [2560, 2560], P('dp', 'tensor'), may hold values from -0.125 to 0.125
- b_recur: bfloat16 [10, 256], P('tensor', 'dp'), may hold values from -3 to 3
- conv_kernel: bfloat16 [4, 10, 256], P(None, 'tensor', 'dp'), may hold values from -3 to 3
- conv_bias: bfloat16 [10, 256], P('tensor', 'dp'), may hold values from -2 to 2
- input_gate_weight: bfloat16 [10, 256, 256], P('tensor', 'dp'), may hold values from -0.375 to 0.375
- input_gate_bias: bfloat16 [10, 256], P('tensor', 'dp'), may hold values from -3 to 3
- decay_gate_weight: bfloat16 [10, 256, 256], P('tensor', 'dp'), may hold values from -0.375 to 0.375
- decay_gate_bias: bfloat16 [10, 256], P('tensor', 'dp'), may hold values from -3 to 3
- decay_base: bfloat16 [10, 256], P('tensor', 'dp'), may hold values from -10 to -5
- w_output: bfloat16 [2560, 2560], P('dp', 'tensor'), may hold values from -0.5 to 0.5
- b_output: bfloat16 [2560], P('dp'), may hold values from -2 to 2
- ffn_gain: bfloat16 [2560], P('dp'), may hold values from -0.5 to 0.5
- w_expand: bfloat16 [2, 2560, 7680], P(None, 'dp', 'tensor'), may hold values from -0.125 to 0.125
- b_expand: bfloat16 [2, 30, 256], P(None, 'tensor', 'dp'), may hold values from -2 to 2
- w_shrink: bfloat16 [2560, 7680], P('dp', 'tensor'), may hold values from -0.125 to 0.125
- b_shrink: bfloat16 [2560], P('dp'), may hold values from -2 to 2
Outputs:
- block_output: bfloat16 [32, 192, 2560], P(None, 'dp')
- input_grad: bfloat16 [32, 192, 2560], P(None, 'dp')
- grad_pre_gain: float32 [2560], P('dp')
- grad_w_branch: float32 [2560, 2560], P('dp', 'tensor')
- grad_b_branch: float32 [10, 256], P('tensor', 'dp')
- grad_w_recur: float32 [2560, 2560], P('dp', 'tensor')
- grad_b_recur: float32 [10, 256], P('tensor', 'dp')
- grad_conv_kernel: float32 [4, 10, 256], P(None, 'tensor', 'dp')
- grad_conv_bias: float32 [10, 256], P('tensor', 'dp')
- grad_w_inlet: float32 [10, 256, 256], P('tensor', 'dp')
- grad_b_inlet: float32 [10, 256], P('tensor', 'dp')
- grad_w_decay: float32 [10, 256, 256], P('tensor', 'dp')
- grad_b_decay: float32 [10, 256], P('tensor', 'dp')
- grad_decay_base: float32 [10, 256], P('tensor', 'dp')
- grad_w_output: float32 [2560, 2560], P('dp', 'tensor')
- grad_b_output: float32 [2560], P('dp')
- grad_ffn_gain: float32 [2560], P('dp')
- grad_w_expand: float32 [2, 2560, 7680], P(None, 'dp', 'tensor')
- grad_b_expand: float32 [2, 30, 256], P(None, 'tensor', 'dp')
- grad_w_shrink: float32 [2560, 7680], P('dp', 'tensor')
- grad_b_shrink: float32 [2560], P('dp')
The draws below stay inside these ranges and needn't reach their ends.
Inputs may be any that keep to these rules, and one draw needn't show every extreme that they name: `seq_lengths`: the longest sequence fills all 192 slots.
All inputs are finite; a program needn't handle non-finite values.
Results may differ from the reference program's by a relative error of at most 0.014.
Values may be sent and summed in bfloat16 or wider, within the bound.
No kernel may reach another device: no remote copies, remote signals or barrier semaphores. Data moves between devices by JAX's collectives and lax.ppermute only.
A program may use at most 576 MiB of HBM per device.

```python
import math
import jax
import jax.numpy as jnp
import numpy as np
from jax import lax

D = 2560
L = 2560
H = 10
FF = 7680
CONV = 4
SLOT = 192
HS = 256
SEQS = 32


def block_scale(rng, shape, split, low, top_value):
    def one(axis_at, shards_of):
        steps = jax.random.uniform(jax.random.fold_in(jax.random.fold_in(rng, 6), axis_at), (shards_of,), jnp.float32, low / len(split), top_value / len(split))
        return jnp.repeat(jnp.exp(steps), shape[axis_at] // shards_of).reshape((-1,) + (1,) * (len(shape) - axis_at - 1))

    level = one(*split[0])
    for cut in split[1:]:
        level = level * one(*cut)
    return level


def profile(count, total, most, lean):
    weights = [(1 << 20) // math.isqrt(grade ** lean) + 1 for grade in range(2, count + 1)]
    spare, holding = total - most - (count - 1), [1] * (count - 1)
    while spare > 0:
        free = [i for i in range(count - 1) if holding[i] < most]
        mass, left = sum([weights[i] for i in free]), spare
        for i in free:
            more = min(most - holding[i], max(1, left * weights[i] // mass), spare)
            holding[i] = holding[i] + more
            spare = spare - more
    return np.array([most] + holding)


def uneven_parts(stream_key, number_of, total, most, skew):
    if number_of == 2:
        one = jax.random.randint(stream_key, (), max(1, total - most), min(most, total - 1) + 1)
        return jnp.stack([one, total - one])
    sizes = jnp.asarray(profile(number_of, total, most, skew), jnp.int32)
    couples = (number_of - 1) // 2
    donor, sink = sizes[1:1 + 2 * couples:2], sizes[2:2 + 2 * couples:2]
    room = jnp.minimum(donor - 1, most - sink)
    moved = jax.random.randint(jax.random.fold_in(stream_key, 1), (couples,), 0, 1 << 20) % (room + 1)
    sizes = sizes.at[1:1 + 2 * couples:2].set(donor - moved).at[2:2 + 2 * couples:2].set(sink + moved)
    return sizes[jax.random.permutation(jax.random.fold_in(stream_key, 2), number_of)]


def scatter_about(rng, dims, spread, most, split=(), held_as=jnp.bfloat16):
    values = spread * jax.random.normal(rng, dims, jnp.float32)
    if split:
        values = values * block_scale(rng, dims, split, -0.22, 0.18)
    return jnp.clip(values, -most, most).astype(held_as)


def setup_inputs(seed: int = 0) -> dict:
    key_list = jax.random.split(jax.random.key(seed), 23)
    block_input = scatter_about(key_list[0], (SEQS, SLOT, D), 1.0, 6.0, ((1, 16),))
    cotangent = scatter_about(key_list[1], (SEQS, SLOT, D), 1.0, 6.0, ((1, 16),))
    seq_lengths = uneven_parts(key_list[2], SEQS, SEQS * SLOT * 3 // 4, SLOT, 2).astype(jnp.int32)
    pre_gain = jnp.clip(jax.random.uniform(key_list[3], (D,), jnp.float32, -0.5, 0.5) * block_scale(key_list[3], (D,), ((0, 16),), -0.4, 0.0), -0.5, 0.5).astype(jnp.bfloat16)
    w_branch = scatter_about(key_list[4], (D, L), D ** -0.5, 0.125, ((0, 16), (1, 2)))
    b_branch = scatter_about(key_list[5], (H, HS), 0.5, 3.0, ((0, 2), (1, 16)))
    w_recur = scatter_about(key_list[6], (D, L), D ** -0.5, 0.125, ((0, 16), (1, 2)))
    b_recur = scatter_about(key_list[7], (H, HS), 0.5, 3.0, ((0, 2), (1, 16)))
    conv_kernel = scatter_about(key_list[8], (CONV, H, HS), CONV ** -0.5, 3.0, ((1, 2), (2, 16)))
    conv_bias = scatter_about(key_list[9], (H, HS), 0.3, 2.0, ((0, 2), (1, 16)))
    input_gate_weight = scatter_about(key_list[10], (H, HS, HS), HS ** -0.5, 0.375, ((0, 2), (1, 16)))
    input_gate_bias = scatter_about(key_list[11], (H, HS), 0.5, 3.0, ((0, 2), (1, 16)))
    decay_gate_weight = scatter_about(key_list[12], (H, HS, HS), HS ** -0.5, 0.375, ((0, 2), (1, 16)))
    decay_gate_bias = scatter_about(key_list[13], (H, HS), 0.5, 3.0, ((0, 2), (1, 16)))
    decay_base = jnp.clip(-10.0 + 5.0 * jax.random.uniform(key_list[14], (H, HS), jnp.float32) ** block_scale(key_list[14], (H, HS), ((0, 2), (1, 16)), -0.2, 0.2), -10.0, -5.0).astype(jnp.bfloat16)
    w_output = scatter_about(key_list[15], (D, L), (L // 16) ** -0.5, 0.5, ((0, 16), (1, 2)))
    b_output = scatter_about(key_list[16], (D,), 0.3, 2.0, ((0, 16),))
    ffn_gain = jnp.clip(jax.random.uniform(key_list[17], (D,), jnp.float32, -0.5, 0.5) * block_scale(key_list[17], (D,), ((0, 16),), -0.4, 0.0), -0.5, 0.5).astype(jnp.bfloat16)
    w_expand = scatter_about(key_list[18], (2, D, FF), D ** -0.5, 0.125, ((1, 16), (2, 2)))
    b_expand = scatter_about(key_list[19], (2, FF // HS, HS), 0.3, 2.0, ((1, 2), (2, 16)))
    w_shrink = scatter_about(key_list[20], (D, FF), (FF // 4) ** -0.5, 0.125, ((0, 16), (1, 2)))
    b_shrink = scatter_about(key_list[21], (D,), 0.3, 2.0, ((0, 16),))
    return dict(block_input=block_input, cotangent=cotangent, seq_lengths=seq_lengths, pre_gain=pre_gain, w_branch=w_branch, b_branch=b_branch, w_recur=w_recur, b_recur=b_recur, conv_kernel=conv_kernel, conv_bias=conv_bias, input_gate_weight=input_gate_weight, input_gate_bias=input_gate_bias, decay_gate_weight=decay_gate_weight, decay_gate_bias=decay_gate_bias, decay_base=decay_base, w_output=w_output, b_output=b_output, ffn_gain=ffn_gain, w_expand=w_expand, b_expand=b_expand, w_shrink=w_shrink, b_shrink=b_shrink)


EXACT_PRECISION = lax.Precision.HIGHEST

@jax.custom_vjp
def low(v):
    return lax.optimization_barrier(v.astype(jnp.bfloat16)).astype(jnp.float32)

@jax.custom_vjp
def reduced_backward(v):
    return v

def low_keep(v):
    return (low(v), None)

def low_pass(kept, grad):
    return (grad,)

def back_keep(v):
    return (v, None)

def back_low(kept, grad):
    return (low(grad),)
low.defvjp(low_keep, low_pass)
reduced_backward.defvjp(back_keep, back_low)

def rms_norm(values, gain_vec):
    return values * lax.rsqrt(lax.optimization_barrier(jnp.mean(values * values, axis=-1, keepdims=True)) + 1e-06) * (1.0 + gain_vec)

def causal_conv(values, kernel, offset_bias):
    taps = kernel.shape[0]
    length = values.shape[1]
    padded = jnp.pad(values, ((0, 0), (taps - 1, 0), (0, 0)))
    summed = offset_bias + jnp.zeros_like(values)
    for offset in range(taps):
        summed = summed + kernel[offset] * padded[:, taps - 1 - offset:taps - 1 - offset + length]
    return summed

def combine(earlier, later):
    return (earlier[0] * later[0], later[0] * earlier[1] + later[1])

def recurrence(decays, source):
    return lax.associative_scan(combine, (decays, source), axis=1)[1]

def lru_core(branch_pre, conv_out, input_preactivation, decay_preactivation, decay_vec):
    inlet_gate = jax.nn.sigmoid(input_preactivation)
    forget = jax.nn.sigmoid(decay_preactivation)
    log_decay = -8.0 * forget * jax.nn.softplus(decay_vec)
    decays = jnp.exp(log_decay)
    input_scale = jnp.sqrt(jnp.maximum(1.0 - jnp.exp(2.0 * log_decay), 0.001))
    first_row = lax.broadcasted_iota(jnp.int32, conv_out.shape, 1) == 0
    input_scale = jnp.where(first_row, 1.0, input_scale)
    states = recurrence(decays, conv_out * inlet_gate * input_scale)
    return jax.nn.gelu(branch_pre, approximate=True) * states

def forward(inputs, row_mask, weights):
    pre_gain, w_branch, b_branch, w_recur, b_recur, conv_kernel, conv_bias, input_gate_weight, input_gate_bias, decay_gate_weight, decay_gate_bias, decay_base, w_output, b_output, ffn_gain, w_expand, b_expand, w_shrink, b_shrink = weights
    seq_count, length, model_width = inputs.shape
    head_count, head_size = input_gate_bias.shape
    channels = head_count * head_size
    normed = low(rms_norm(inputs, pre_gain))
    branch_pre = reduced_backward(jnp.einsum('spd,dc->spc', normed, w_branch, precision=EXACT_PRECISION) + b_branch.reshape(channels))
    recur_pre = reduced_backward(jnp.einsum('spd,dc->spc', normed, w_recur, precision=EXACT_PRECISION) + b_recur.reshape(channels))
    conv_out = causal_conv(recur_pre, conv_kernel.reshape(-1, channels), conv_bias.reshape(channels))
    convolved_heads = low(conv_out).reshape(seq_count, length, head_count, head_size)
    input_preactivation = reduced_backward(jnp.einsum('zjmf,mfk->zjmk', convolved_heads, input_gate_weight, precision=EXACT_PRECISION) + input_gate_bias)
    decay_preactivation = reduced_backward(jnp.einsum('zjmf,mfk->zjmk', convolved_heads, decay_gate_weight, precision=EXACT_PRECISION) + decay_gate_bias)
    mixed = low(lru_core(branch_pre, conv_out, input_preactivation.reshape(seq_count, length, channels), decay_preactivation.reshape(seq_count, length, channels), decay_base.reshape(channels)))
    branch_out = reduced_backward(jnp.einsum('spc,dc->spd', mixed, w_output, precision=EXACT_PRECISION) + b_output)
    middle = inputs + branch_out
    second = low(rms_norm(middle, ffn_gain))
    gate_pre = reduced_backward(jnp.einsum('spd,df->spf', second, w_expand[0], precision=EXACT_PRECISION) + b_expand[0].reshape(-1))
    up_pre = reduced_backward(jnp.einsum('spd,df->spf', second, w_expand[1], precision=EXACT_PRECISION) + b_expand[1].reshape(-1))
    hidden = low(jax.nn.gelu(gate_pre, approximate=True) * up_pre)
    ffn_out = reduced_backward(jnp.einsum('spf,df->spd', hidden, w_shrink, precision=EXACT_PRECISION) + b_shrink)
    return row_mask * (middle + ffn_out)

def reference(block_input, cotangent, seq_lengths, pre_gain, w_branch, b_branch, w_recur, b_recur, conv_kernel, conv_bias, input_gate_weight, input_gate_bias, decay_gate_weight, decay_gate_bias, decay_base, w_output, b_output, ffn_gain, w_expand, b_expand, w_shrink, b_shrink):
    params = tuple((weight.astype(jnp.float32) for weight in (pre_gain, w_branch, b_branch, w_recur, b_recur, conv_kernel, conv_bias, input_gate_weight, input_gate_bias, decay_gate_weight, decay_gate_bias, decay_base, w_output, b_output, ffn_gain, w_expand, b_expand, w_shrink, b_shrink)))
    seq_count = block_input.shape[0]
    group_size = min(16, seq_count)
    blocks = seq_count // group_size
    inputs = block_input.astype(jnp.float32).reshape(blocks, group_size, SLOT, D)
    upstream = cotangent.astype(jnp.float32).reshape(blocks, group_size, SLOT, D)
    lengths = seq_lengths.reshape(blocks, group_size)

    def one_block(totals, pieces):
        values, grads_out, limits = pieces
        row_mask = (lax.broadcasted_iota(jnp.int32, (group_size, SLOT), 1) < limits[:, None]).astype(jnp.float32)[..., None]

        def apply_block(inner, weights):
            return forward(inner, row_mask, weights)
        result, pullback = jax.vjp(apply_block, values, params)
        grad_inner, weight_grads = pullback(grads_out)
        return (jax.tree.map(jnp.add, totals, weight_grads), (result, grad_inner))
    totals, (results, grad_inputs) = lax.scan(one_block, jax.tree.map(jnp.zeros_like, params), (inputs, upstream, lengths))
    block_output = results.reshape(seq_count, SLOT, D).astype(jnp.bfloat16)
    input_grad = grad_inputs.reshape(seq_count, SLOT, D).astype(jnp.bfloat16)
    return (block_output, input_grad, totals[0], totals[1], totals[2], totals[3], totals[4], totals[5], totals[6], totals[7], totals[8], totals[9], totals[10], totals[11], totals[12], totals[13], totals[14], totals[15], totals[16], totals[17], totals[18])
```

```python
import functools

import jax
import jax.numpy as jnp
from jax import lax
from jax.experimental import pallas as pl
from jax.experimental.pallas import tpu as pltpu
from jax.sharding import Mesh, PartitionSpec as P

F32, BF16 = jnp.float32, jnp.bfloat16
LANES = 128
PLANES = 4
CORES = 2
CHUNKS = 4
DP = ("z", "x", "c")
GELU_A, GELU_B = 0.7978845608028654, 0.044715


def gelu_parts(v):
    square = v * v
    bent = jnp.tanh(GELU_A * v * (1.0 + GELU_B * square))
    half = 0.5 * (1.0 + bent)
    slope = half + 0.5 * v * (1.0 - bent * bent) * (GELU_A * (1.0 + 3.0 * GELU_B * square))
    return v * half, slope


def gelu(v):
    return v * (0.5 * (1.0 + jnp.tanh(GELU_A * v * (1.0 + GELU_B * v * v))))


def dot(a, b, dims=((1,), (0,))):
    return lax.dot_general(a, b, (dims, ((), ())), preferred_element_type=F32)


def logistic(v):
    return 1.0 / (1.0 + jnp.exp(-v))


def input_scale(decay, at_start):
    spare = 1.0 - decay * decay
    scale = jnp.sqrt(jnp.maximum(spare, 0.001))
    return jnp.where(at_start, 1.0, scale), spare


def start_rows(first_ref, rows, seqs, width):
    row = lax.broadcasted_iota(jnp.int32, (rows, width), 0)
    return jnp.logical_and(row < seqs, first_ref[0] == 1)


def gates_kernel(first_ref, r_ref, v_ref, wi_ref, wd_ref, c_ref, si_ref, sd_ref, e_ref, p_ref, *, seqs, taps):
    rows, width = c_ref.shape
    halo = r_ref.shape[0] - rows
    conv = v_ref[taps : taps + 1, :] + v_ref[0:1, :] * r_ref[pl.ds(halo, rows), :]
    for k in range(1, taps):
        conv = conv + v_ref[k : k + 1, :] * r_ref[pl.ds(halo - k * seqs, rows), :]
    c_ref[...] = conv
    low = conv.astype(BF16)
    si = logistic(dot(low, wi_ref[0]) + v_ref[taps + 1 : taps + 2, :])
    sd = logistic(dot(low, wd_ref[0]) + v_ref[taps + 2 : taps + 3, :])
    si_ref[...] = si
    sd_ref[...] = sd
    decay = jnp.exp(sd * v_ref[taps + 3 : taps + 4, :])
    scale, _ = input_scale(decay, start_rows(first_ref, rows, seqs, width))
    source = conv * si * scale
    state, total = source[:seqs], decay[:seqs]
    for p in range(1, rows // seqs):
        a = decay[p * seqs : (p + 1) * seqs]
        state = a * state + source[p * seqs : (p + 1) * seqs]
        total = total * a
    e_ref[...] = state
    p_ref[...] = total


def states_kernel(first_ref, c_ref, si_ref, sd_ref, b_ref, v_ref, carry_ref, s_ref, m_ref, *, seqs, taps):
    rows, width = c_ref.shape
    decay = jnp.exp(sd_ref[...] * v_ref[taps + 3 : taps + 4, :])
    scale, _ = input_scale(decay, start_rows(first_ref, rows, seqs, width))
    source = c_ref[...] * si_ref[...] * scale
    state = carry_ref[...]
    for p in range(rows // seqs):
        at = slice(p * seqs, (p + 1) * seqs)
        state = decay[at] * state + source[at]
        s_ref[pl.ds(p * seqs, seqs), :] = state
    m_ref[...] = (gelu(b_ref[...]) * s_ref[...]).astype(BF16)


def branch_kernel(dm_ref, b_ref, s_ref, sd_ref, v_ref, t_ref, db_ref, e_ref, sum_ref, *, seqs, taps):
    rows, _ = t_ref.shape
    value, slope = gelu_parts(b_ref[...])
    dm = dm_ref[...]
    t = dm * value
    t_ref[...] = t
    db = (dm * s_ref[...] * slope).astype(BF16)
    db_ref[...] = db
    sum_ref[...] = jnp.broadcast_to(jnp.sum(db.astype(F32), axis=0, keepdims=True), sum_ref.shape)
    decay = jnp.exp(sd_ref[...] * v_ref[taps + 3 : taps + 4, :])
    count = rows // seqs
    grad = t[(count - 1) * seqs :]
    for p in range(count - 2, -1, -1):
        grad = t[p * seqs : (p + 1) * seqs] + decay[(p + 1) * seqs : (p + 2) * seqs] * grad
    e_ref[...] = decay[:seqs] * grad


def core_kernel(
    first_ref, t_ref, c_ref, si_ref, sd_ref, s_ref, r_ref, v_ref, carry_ref, late_ref, wi_ref, wd_ref,
    dc_ref, gi_ref, gd_ref, sum_ref, ds_ref, *, seqs, taps,
):
    rows, width = c_ref.shape
    halo = r_ref.shape[0] - rows
    count = rows // seqs
    si, sd, conv = si_ref[...], sd_ref[...], c_ref[...]
    rate = v_ref[taps + 3 : taps + 4, :]
    decay = jnp.exp(sd * rate)
    at_start = start_rows(first_ref, rows, seqs, width)
    scale, spare = input_scale(decay, at_start)
    grad = late_ref[...]
    for p in range(count - 1, -1, -1):
        grad = t_ref[pl.ds(p * seqs, seqs), :] + grad
        ds_ref[pl.ds(p * seqs, seqs), :] = grad
        grad = decay[p * seqs : (p + 1) * seqs] * grad
    ds = ds_ref[...]
    before = carry_ref[...] if count == 1 else jnp.concatenate([carry_ref[...], s_ref[pl.ds(0, rows - seqs), :]], axis=0)
    bends = jnp.logical_and(spare > 0.001, jnp.logical_not(at_start))
    d_scale = jnp.where(bends, -(decay * decay) / scale, 0.0)
    gated = ds * conv
    d_log = ds * before * decay + gated * si * d_scale
    d_in = (gated * scale * si * (1.0 - si)).astype(BF16)
    d_dec = (d_log * rate * sd * (1.0 - sd)).astype(BF16)
    low = conv.astype(BF16)
    gi_ref[0] = dot(low, d_in, ((0,), (0,))).astype(gi_ref.dtype)
    gd_ref[0] = dot(low, d_dec, ((0,), (0,))).astype(gd_ref.dtype)
    dc = ds * si * scale + dot(d_in, wi_ref[0], ((1,), (1,))) + dot(d_dec, wd_ref[0], ((1,), (1,)))
    dc_ref[...] = dc

    def total(values):
        return jnp.sum(values, axis=0, keepdims=True)

    parts = [
        total(d_in.astype(F32)),
        total(d_dec.astype(F32)),
        total(d_log * sd) * v_ref[taps + 4 : taps + 5, :],
        total(dc),
    ]
    for k in range(taps):
        parts.append(total(r_ref[pl.ds(halo - k * seqs, rows), :] * dc))
    sum_ref[...] = jnp.concatenate(parts, axis=0)


def head_calls(heads, width, rows, halo_rows, seqs, taps):
    def cols(n):
        return pl.BlockSpec((n, width), lambda h: (0, h))

    flag = pl.BlockSpec(memory_space=pltpu.SMEM)
    mats = pl.BlockSpec((1, width, width), lambda h: (h, 0, 0))
    full = heads * width
    params = pltpu.CompilerParams(vmem_limit_bytes=48 * 1024 * 1024)
    vec_rows = 16

    def shape(n, kind=F32):
        return jax.ShapeDtypeStruct((n, full), kind)

    def call(kernel, ins, outs, shapes, scratch=(), flops=0):
        return pl.pallas_call(
            functools.partial(kernel, seqs=seqs, taps=taps),
            grid=(heads,),
            in_specs=ins,
            out_specs=outs,
            out_shape=shapes,
            scratch_shapes=list(scratch),
            compiler_params=params,
            cost_estimate=pl.CostEstimate(flops=flops, bytes_accessed=rows * full * 4 * len(ins), transcendentals=4 * rows * full),
        )

    unit = 2 * rows * full * width
    return (
        call(
            gates_kernel,
            [flag, cols(halo_rows), cols(vec_rows), mats, mats],
            [cols(rows), cols(rows), cols(rows), cols(seqs), cols(seqs)],
            [shape(rows), shape(rows), shape(rows), shape(seqs), shape(seqs)],
            flops=2 * unit,
        ),
        call(
            states_kernel,
            [flag, cols(rows), cols(rows), cols(rows), cols(rows), cols(vec_rows), cols(seqs)],
            [cols(rows), cols(rows)],
            [shape(rows), shape(rows, BF16)],
        ),
        call(
            branch_kernel,
            [cols(rows), cols(rows), cols(rows), cols(rows), cols(vec_rows)],
            [cols(rows), cols(rows), cols(seqs), cols(8)],
            [shape(rows), shape(rows, BF16), shape(seqs), shape(8)],
        ),
        call(
            core_kernel,
            [flag, cols(rows), cols(rows), cols(rows), cols(rows), cols(rows), cols(halo_rows), cols(vec_rows),
             cols(seqs), cols(seqs), mats, mats],
            [cols(rows), mats, mats, cols(4 + taps)],
            [shape(rows), jax.ShapeDtypeStruct((heads, width, width), BF16),
             jax.ShapeDtypeStruct((heads, width, width), BF16), shape(4 + taps)],
            scratch=[pltpu.VMEM((rows, width), F32)],
            flops=4 * unit,
        ),
    )


def swap(v, axis):
    return lax.ppermute(v, axis, [(0, 1), (1, 0)])


def gather_rows(v, axis):
    if lax.axis_size(axis) == 2:
        return jnp.concatenate([v, swap(v, axis)], axis=0)
    return lax.all_gather(v, axis, axis=0, tiled=True)


def scatter_rows(v, axis):
    count = lax.axis_size(axis)
    if count == 2:
        half = v.shape[0] // 2
        return v[:half].astype(F32) + swap(v[half:].astype(BF16), axis).astype(F32)
    return lax.psum_scatter(v.astype(BF16), axis, scatter_dimension=0, tiled=True).astype(F32)


def halves(v, axis):
    half = v.shape[0] // 2
    at = lax.axis_index(axis)
    own = lax.dynamic_slice_in_dim(v, at * half, half, 0)
    return own, lax.dynamic_slice_in_dim(v, (1 - at) * half, half, 0)


def whole_rows(own, axis):
    other = swap(own, axis)
    low = lax.axis_index(axis) == 0
    return jnp.concatenate([jnp.where(low, own, other), jnp.where(low, other, own)], axis=0)


def ranks(value, axis):
    count = lax.axis_size(axis)
    if count == 2:
        other = swap(value, axis)
        low = lax.axis_index(axis) == 0
        return [jnp.where(low, value, other), jnp.where(low, other, value)]
    every = lax.all_gather(value, axis)
    return [every[j] for j in range(count)]


def carry_in(state, total, backward):
    pair = jnp.stack([state, total])
    inner = []
    for axis, kind in (("c", F32), ("x", BF16)):
        parts = [part.astype(F32) for part in ranks(pair.astype(kind), axis)]
        order = range(len(parts))
        at = lax.axis_index(axis)
        if backward:
            order, at = [len(parts) - 1 - j for j in order], len(parts) - 1 - at
        gone = jnp.stack([jnp.zeros_like(state), jnp.ones_like(total)])
        mine = gone
        for place, j in enumerate(order):
            mine = jnp.where(at == place, gone, mine)
            gone = jnp.stack([parts[j][0] + parts[j][1] * gone[0], parts[j][1] * gone[1]])
        inner.append(mine)
        pair = gone
    planes = lax.axis_size("z")
    sent = pair.astype(BF16)
    entering = jnp.zeros_like(state)
    steps = []
    for far in range(1, planes):
        if backward:
            route = [(j + far, j) for j in range(planes - far)]
        else:
            route = [(j, j + far) for j in range(planes - far)]
        steps.append(lax.ppermute(sent if far < planes - 1 else sent[:1], "z", route).astype(F32))
    for step in reversed(steps):
        entering = step[0] + (step[1] * entering if step.shape[0] == 2 else 0.0)
    for mine in reversed(inner):
        entering = mine[0] + mine[1] * entering
    return entering


def norm(v, gain):
    scale = lax.rsqrt(jnp.mean(v * v, axis=-1, keepdims=True) + 1e-6)
    return v * scale * gain, scale


def norm_back(v, scale, gain, d_out):
    scaled = gain * d_out
    mean = jnp.mean(v * scaled, axis=-1, keepdims=True)
    return scale * scaled - v * (scale * scale * scale * mean), jnp.sum(v * scale * d_out, axis=0)


def body(
    block_input, cotangent, seq_lengths, pre_gain, w_branch, b_branch, w_recur, b_recur, conv_kernel, conv_bias,
    input_gate_weight, input_gate_bias, decay_gate_weight, decay_gate_bias, decay_base, w_output, b_output,
    ffn_gain, w_expand, b_expand, w_shrink, b_shrink,
):
    mid = lax.axis_size("x")
    groups = PLANES * mid * CORES
    place = lax.axis_index(DP)
    side = lax.axis_index("y")
    seqs, pieces, width = block_input.shape
    rows = seqs * pieces
    taps, heads, head_part = conv_kernel.shape
    head_size = head_part * groups
    channels = heads * head_size
    part = w_recur.shape[0]
    units = w_shrink.shape[1]
    halo = (taps - 1) * seqs

    x_low = block_input.transpose(1, 0, 2).reshape(rows, width)
    positions = place * pieces + lax.broadcasted_iota(jnp.int32, (pieces, seqs), 0)
    mask = (positions < seq_lengths[None, :]).reshape(rows, 1)
    d_out = jnp.where(mask, cotangent.transpose(1, 0, 2).reshape(rows, width), 0).astype(BF16)
    early = lax.ppermute(x_low[rows - halo :], DP, [(j, j + 1) for j in range(groups - 1)])

    vectors = [b_branch, b_recur, *[conv_kernel[k] for k in range(taps)], conv_bias, input_gate_bias,
               decay_gate_bias, decay_base]
    flat = jnp.concatenate([v.reshape(-1) for v in vectors] + [pre_gain, b_output, ffn_gain, b_shrink, b_expand.reshape(-1)])
    small_rows = -(-flat.size // channels)
    pad_rows = -(-small_rows // 16) * 16
    flat = jnp.pad(flat, (0, pad_rows * channels - flat.size)).reshape(pad_rows, channels)
    gate_rows = input_gate_weight.transpose(1, 0, 2).reshape(head_part, channels)
    decay_rows = decay_gate_weight.transpose(1, 0, 2).reshape(head_part, channels)
    packed = jnp.concatenate([w_recur, w_branch, w_output, gate_rows, decay_rows, flat], axis=0)
    gathered = lax.all_gather(packed, DP, axis=0, tiled=False)
    recur_full = gathered[:, :part].reshape(width, channels)
    branch_full = gathered[:, part : 2 * part].reshape(width, channels)
    output_full = gathered[:, 2 * part : 3 * part].reshape(width, channels)

    def gate_full(at):
        return (
            gathered[:, at : at + head_part].reshape(groups, head_part, heads, head_size)
            .transpose(2, 0, 1, 3).reshape(heads, head_size, head_size)
        )

    inlet_full, decay_full = gate_full(3 * part), gate_full(3 * part + head_part)
    every = gathered[:, 3 * part + 2 * head_part :].reshape(groups, -1)[:, : small_rows * channels].astype(F32)
    taken = 0

    def take(count):
        nonlocal taken
        taken += count
        return every[:, taken - count : taken]

    def by_head():
        return take(heads * head_part).reshape(groups, heads, head_part).transpose(1, 0, 2).reshape(channels)

    vec_branch, vec_recur = by_head(), by_head()
    vec_taps = [by_head() for _ in range(taps)]
    vec_conv, vec_inlet, vec_decay, vec_base = by_head(), by_head(), by_head(), by_head()
    gain_one, vec_output, gain_two, vec_shrink = [take(part).reshape(width) for _ in range(4)]
    blocks = b_expand.shape[1]
    vec_expand = take(2 * blocks * head_part).reshape(groups, 2, blocks, head_part).transpose(1, 2, 0, 3).reshape(2, units)
    gain_one, gain_two = 1.0 + gain_one, 1.0 + gain_two
    coefs = jnp.stack(
        vec_taps + [vec_conv, vec_inlet, vec_decay, -8.0 * jax.nn.softplus(vec_base), -8.0 * jax.nn.sigmoid(vec_base)]
    )
    coefs = jnp.pad(coefs, ((0, 16 - coefs.shape[0]), (0, 0)))

    slices = mid * CORES
    tiles = units // LANES
    wide_tiles = -(-tiles // slices)
    wide = wide_tiles * LANES
    starts = [j * (tiles - wide_tiles) // (slices - 1) for j in range(slices)]
    owned = [(starts[j + 1] if j + 1 < slices else tiles) - starts[j] for j in range(slices)]
    chunks = CHUNKS if wide % (CHUNKS * LANES) == 0 else 1
    step = wide // chunks
    sent = []
    for k in range(chunks):
        for j in range(slices):
            at = starts[j] * LANES + k * step
            sent.append(jnp.concatenate([w_expand[0, :, at : at + step], w_expand[1, :, at : at + step], w_shrink[:, at : at + step]], axis=1))
    sent = jnp.stack(sent).reshape(chunks, slices, part, 3 * step)
    held = lax.all_to_all(sent, ("x", "c"), split_axis=1, concat_axis=1, tiled=True)
    held = held.reshape(chunks, slices * part, 3 * step)
    my_slice = lax.axis_index(("x", "c"))
    my_start = jnp.array(starts, jnp.int32)[my_slice] * LANES
    my_owned = jnp.array(owned, jnp.int32)[my_slice] * LANES
    held, gathered_after = lax.optimization_barrier((held, output_full))
    output_full = gathered_after
    ffn_full = [lax.all_gather(held[k], "z", axis=0, tiled=True) for k in range(chunks)]
    my_bias = lax.dynamic_slice_in_dim(vec_expand, my_start, wide, 1)

    d_first, d_second = halves(d_out, "y")
    d_plane = gather_rows(gather_rows(jnp.concatenate([d_first, d_second], axis=0), "x"), "c")

    gates, states, branch_back, core_back = head_calls(heads, head_size, rows, rows + halo, seqs, taps)
    first = (place == 0).astype(jnp.int32).reshape(1)
    x_ext = jnp.concatenate([early, x_low], axis=0).astype(F32)
    normed_f, _ = norm(x_ext, gain_one)
    normed_ext = normed_f.astype(BF16)
    normed = normed_ext[halo:]
    recur = dot(normed_ext, recur_full) + vec_recur
    ext_row = lax.broadcasted_iota(jnp.int32, (rows + halo, 1), 0)
    recur = jnp.where(jnp.logical_and(ext_row < halo, place == 0), 0.0, recur)
    conv, sig_in, sig_dec, end, total = gates(first, recur, coefs, inlet_full, decay_full)
    carry = carry_in(end, total, False)
    branch = dot(normed, branch_full) + vec_branch
    state, mixed = states(first, conv, sig_in, sig_dec, branch, coefs, carry)
    out_own, out_other = halves(dot(mixed, output_full, ((1,), (1,))), "y")
    x_own, _ = halves(x_low, "y")
    x_own = x_own.astype(F32)
    middle = x_own + out_own + swap(out_other.astype(BF16), "y").astype(F32) + vec_output
    second_f, scale_two = norm(middle, gain_two)
    second = second_f.astype(BF16)

    plane = gather_rows(gather_rows(gather_rows(second, "y"), "x"), "c")
    ffn_out = 0.0
    d_second_part = 0.0
    ffn_grads, bias_grads = [], []
    for k in range(chunks):
        weights = ffn_full[k]
        pre = dot(plane, weights[:, : 2 * step])
        gate = pre[:, :step] + my_bias[0, k * step : (k + 1) * step]
        up = pre[:, step:] + my_bias[1, k * step : (k + 1) * step]
        d_hidden = dot(d_plane, weights[:, 2 * step :])
        mine = k * step + lax.broadcasted_iota(jnp.int32, (1, step), 1) < my_owned
        value, slope = gelu_parts(gate)
        hidden = jnp.where(mine, value * up, 0.0).astype(BF16)
        d_gate = jnp.where(mine, d_hidden * up * slope, 0.0).astype(BF16)
        d_up = jnp.where(mine, d_hidden * value, 0.0).astype(BF16)
        d_pre = jnp.concatenate([d_gate, d_up], axis=1)
        d_second_part = d_second_part + dot(d_pre, weights[:, : 2 * step], ((1,), (1,)))
        ffn_out = ffn_out + dot(hidden, weights[:, 2 * step :], ((1,), (1,)))
        grads = jnp.concatenate(
            [dot(plane, d_pre, ((0,), (0,))).astype(BF16), dot(d_plane, hidden, ((0,), (0,))).astype(BF16)], axis=1
        )
        ffn_grads.append(lax.psum_scatter(grads, "z", scatter_dimension=0, tiled=True))
        bias_grads.append(jnp.sum(d_pre.astype(F32), axis=0).reshape(2, step))

    def to_owner(values):
        values = values.astype(BF16)
        return scatter_rows(scatter_rows(scatter_rows(values, "c").astype(BF16), "x").astype(BF16), "y")

    d_second_own = to_owner(d_second_part)
    d_middle, grad_gain_two = norm_back(middle, scale_two, gain_two, d_second_own)
    d_middle = d_middle + d_first.astype(F32)
    d_low_own = d_middle.astype(BF16)
    mask_own, _ = halves(mask, "y")
    result = jnp.where(mask_own, middle + to_owner(ffn_out) + vec_shrink, 0.0).astype(BF16)
    result = whole_rows(result, "y")

    d_low = whole_rows(d_low_own, "y")
    d_mixed = dot(d_low, output_full)
    pulled, d_branch, end_back, branch_sum = branch_back(d_mixed, branch, state, sig_dec, coefs)
    late = carry_in(end_back, total, True)
    grad_output = dot(d_low, mixed, ((0,), (0,))).astype(BF16)
    grad_branch = dot(normed, d_branch, ((0,), (0,))).astype(BF16)
    d_conv, grad_inlet, grad_decay, core_sums = core_back(
        first, pulled, conv, sig_in, sig_dec, state, recur, coefs, carry, late, inlet_full, decay_full
    )
    after = lax.ppermute(d_conv[:halo].astype(BF16), DP, [(j + 1, j) for j in range(groups - 1)])
    d_ext = jnp.concatenate([d_conv, after.astype(F32)], axis=0)
    d_recur = vec_taps[0] * d_ext[:rows]
    for k in range(1, taps):
        d_recur = d_recur + vec_taps[k] * d_ext[k * seqs : k * seqs + rows]
    d_recur = d_recur.astype(BF16)
    grad_recur = dot(normed, d_recur, ((0,), (0,))).astype(BF16)
    d_normed = dot(d_branch, branch_full, ((1,), (1,))) + dot(d_recur, recur_full, ((1,), (1,)))
    dn_own, dn_other = halves(d_normed, "y")
    dn_own = dn_own + swap(dn_other.astype(BF16), "y").astype(F32)
    scale_one = lax.rsqrt(jnp.mean(x_own * x_own, axis=-1, keepdims=True) + 1e-6)
    d_input, grad_gain_one = norm_back(x_own, scale_one, gain_one, dn_own)
    d_input = whole_rows((d_middle + d_input).astype(BF16), "y")

    shared = jnp.stack([grad_gain_one, jnp.sum(d_low_own.astype(F32), axis=0), grad_gain_two])
    shared = shared + swap(shared, "y")
    shared = jnp.concatenate([shared, jnp.sum(d_out.astype(F32), axis=0)[None]], axis=0)
    recur_sum = jnp.sum(d_recur.astype(F32), axis=0)
    by_channel = jnp.concatenate(
        [branch_sum[:1], recur_sum[None], core_sums[4:], core_sums[3:4], core_sums[:3]], axis=0
    )
    by_channel = by_channel.reshape(-1, heads, groups, head_part).transpose(2, 0, 1, 3).reshape(groups, -1)
    by_feature = shared.reshape(4, groups, part).transpose(1, 0, 2).reshape(groups, -1)
    by_unit = lax.dynamic_update_slice_in_dim(jnp.zeros((2, units), F32), jnp.concatenate(bias_grads, axis=1), my_start, 1)
    by_unit = by_unit.reshape(2, blocks, groups, head_part).transpose(2, 0, 1, 3).reshape(groups, -1)
    small = jnp.concatenate([by_channel, by_feature, by_unit], axis=1)
    small_count = small.shape[1]
    small = jnp.pad(small, ((0, 0), (0, pad_rows * channels - small_count))).reshape(groups, pad_rows, channels)

    def gate_pack(grad):
        return grad.reshape(heads, groups, head_part, head_size).transpose(1, 2, 0, 3).reshape(groups, head_part, channels)

    pack_a = jnp.concatenate(
        [grad_output.reshape(groups, part, channels), grad_branch.reshape(groups, part, channels)], axis=1
    )
    pack_b = jnp.concatenate(
        [grad_recur.reshape(groups, part, channels), gate_pack(grad_inlet), gate_pack(grad_decay), small.astype(BF16)], axis=1
    )
    sum_a = lax.psum_scatter(pack_a, DP, scatter_dimension=0, tiled=False).astype(F32)
    sum_b = lax.psum_scatter(pack_b, DP, scatter_dimension=0, tiled=False).astype(F32)

    ffn_sum = jnp.stack(ffn_grads).reshape(chunks, slices, part, 3 * step)
    ffn_sum = lax.all_to_all(ffn_sum, ("x", "c"), split_axis=1, concat_axis=1, tiled=True)
    grads_out = []
    for kind in range(3):
        pieces_out = []
        for j in range(slices):
            for k in range(chunks):
                keep = min(step, owned[j] * LANES - k * step)
                if keep > 0:
                    pieces_out.append(ffn_sum[k, j, :, kind * step : kind * step + keep])
        grads_out.append(jnp.concatenate(pieces_out, axis=1).astype(F32))
    grad_expand = jnp.stack(grads_out[:2])
    grad_shrink = grads_out[2]

    given = sum_b[part + 2 * head_part :].reshape(-1)[:small_count]
    taken = 0

    def give(*dims):
        nonlocal taken
        count = 1
        for n in dims:
            count *= n
        taken += count
        return given[taken - count : taken].reshape(dims)

    head_dims = (heads, head_part)
    g_b_branch, g_b_recur, g_kernel = give(*head_dims), give(*head_dims), give(taps, *head_dims)
    g_conv_bias, g_b_inlet, g_b_decay, g_base = give(*head_dims), give(*head_dims), give(*head_dims), give(*head_dims)
    g_pre_gain, g_b_output, g_ffn_gain, g_b_shrink = give(part), give(part), give(part), give(part)
    g_b_expand = give(2, blocks, head_part)

    def gate_out(at):
        return sum_b[at : at + head_part].reshape(head_part, heads, head_size).transpose(1, 0, 2)

    def rows_out(v):
        return v.reshape(pieces, seqs, width).transpose(1, 0, 2)

    return (
        rows_out(result), rows_out(d_input), g_pre_gain, sum_a[part:], g_b_branch, sum_b[:part], g_b_recur,
        g_kernel, g_conv_bias, gate_out(part), g_b_inlet, gate_out(part + head_part), g_b_decay, g_base,
        sum_a[:part], g_b_output, g_ffn_gain, grad_expand, g_b_expand, grad_shrink, g_b_shrink,
    )


def solution(mesh):
    groups, sides = mesh.shape["dp"], mesh.shape["tensor"]
    mid = groups // (PLANES * CORES)
    grid = Mesh(mesh.devices.reshape(PLANES, mid, CORES, sides), ("z", "x", "c", "y"))
    rows, vec = P(None, DP, None), P(DP)
    mat, head, tap, gate = P(DP, "y"), P("y", DP), P(None, "y", DP), P("y", DP, None)
    wide = P(None, DP, "y")
    return jax.shard_map(
        body,
        mesh=grid,
        in_specs=(
            rows, rows, P(), vec, mat, head, mat, head, tap, head, gate, head, gate, head, head, mat, vec, vec,
            wide, tap, mat, vec,
        ),
        out_specs=(
            rows, rows, vec, mat, head, mat, head, tap, head, gate, head, gate, head, head, mat, vec, vec,
            wide, tap, mat, vec,
        ),
        check_vma=False,
    )
```

```python
import functools

import jax
import jax.numpy as jnp
from jax import lax
from jax.experimental import pallas as pl
from jax.experimental.pallas import tpu as pltpu
from jax.sharding import Mesh, PartitionSpec as P

F32, BF16 = jnp.float32, jnp.bfloat16
LANES = 128
PLANES = 4
CORES = 2
CHUNKS = 2
VMEM_BYTES = 56 * 1024 * 1024
SMALL = pl.CostEstimate(flops=1, bytes_accessed=1, transcendentals=0)
DP = ("z", "x", "c")
GELU_A, GELU_B = 0.7978845608028654, 0.044715


def gelu_parts(v):
    square = v * v
    bent = jnp.tanh(GELU_A * v * (1.0 + GELU_B * square))
    half = 0.5 * (1.0 + bent)
    slope = half + 0.5 * v * (1.0 - bent * bent) * (GELU_A * (1.0 + 3.0 * GELU_B * square))
    return v * half, slope


def gelu(v):
    return v * (0.5 * (1.0 + jnp.tanh(GELU_A * v * (1.0 + GELU_B * v * v))))


def dot(a, b, dims=((1,), (0,))):
    return lax.dot_general(a, b, (dims, ((), ())), preferred_element_type=F32)


def tie(*values):
    return lax.optimization_barrier(values)


def input_scale(decay, at_start):
    spare = 1.0 - decay * decay
    scale = jnp.sqrt(jnp.maximum(spare, 0.001))
    return jnp.where(at_start, 1.0, scale), spare


def start_rows(first_ref, rows, seqs, width):
    row = lax.broadcasted_iota(jnp.int32, (rows, width), 0)
    return jnp.logical_and(row < seqs, first_ref[0] == 1)


def gates_kernel(first_ref, r_ref, v_ref, wi_ref, wd_ref, c_ref, si_ref, sd_ref, e_ref, p_ref, *, seqs, taps):
    rows, width = c_ref.shape
    halo = r_ref.shape[0] - rows
    conv = v_ref[taps : taps + 1, :] + v_ref[0:1, :] * r_ref[pl.ds(halo, rows), :]
    for k in range(1, taps):
        conv = conv + v_ref[k : k + 1, :] * r_ref[pl.ds(halo - k * seqs, rows), :]
    c_ref[...] = conv
    low = conv.astype(BF16)
    si = jax.nn.sigmoid(dot(low, wi_ref[...]) + v_ref[taps + 1 : taps + 2, :])
    sd = jax.nn.sigmoid(dot(low, wd_ref[...]) + v_ref[taps + 2 : taps + 3, :])
    si_ref[...] = si
    sd_ref[...] = sd
    decay = jnp.exp(sd * v_ref[taps + 3 : taps + 4, :])
    scale, _ = input_scale(decay, start_rows(first_ref, rows, seqs, width))
    source = conv * si * scale
    state, total = source[:seqs], decay[:seqs]
    for p in range(1, rows // seqs):
        a = decay[p * seqs : (p + 1) * seqs]
        state = a * state + source[p * seqs : (p + 1) * seqs]
        total = total * a
    e_ref[...] = state
    p_ref[...] = total


def states_kernel(first_ref, c_ref, si_ref, sd_ref, b_ref, v_ref, carry_ref, s_ref, m_ref, *, seqs, taps):
    rows, width = c_ref.shape
    decay = jnp.exp(sd_ref[...] * v_ref[taps + 3 : taps + 4, :])
    scale, _ = input_scale(decay, start_rows(first_ref, rows, seqs, width))
    source = c_ref[...] * si_ref[...] * scale
    state = carry_ref[...]
    for p in range(rows // seqs):
        at = slice(p * seqs, (p + 1) * seqs)
        state = decay[at] * state + source[at]
        s_ref[pl.ds(p * seqs, seqs), :] = state
    m_ref[...] = (gelu(b_ref[...]) * s_ref[...]).astype(BF16)


def branch_kernel(dm_ref, b_ref, s_ref, sd_ref, v_ref, t_ref, db_ref, e_ref, sum_ref, *, seqs, taps):
    rows, _ = t_ref.shape
    value, slope = gelu_parts(b_ref[...])
    dm = dm_ref[...]
    t = dm * value
    t_ref[...] = t
    db = (dm * s_ref[...] * slope).astype(BF16)
    db_ref[...] = db
    sum_ref[...] = jnp.broadcast_to(jnp.sum(db.astype(F32), axis=0, keepdims=True), sum_ref.shape)
    decay = jnp.exp(sd_ref[...] * v_ref[taps + 3 : taps + 4, :])
    count = rows // seqs
    grad = t[(count - 1) * seqs :]
    for p in range(count - 2, -1, -1):
        grad = t[p * seqs : (p + 1) * seqs] + decay[(p + 1) * seqs : (p + 2) * seqs] * grad
    e_ref[...] = decay[:seqs] * grad


def core_kernel(
    first_ref, t_ref, c_ref, si_ref, sd_ref, s_ref, r_ref, v_ref, carry_ref, late_ref, wi_ref, wd_ref,
    dc_ref, gi_ref, gd_ref, sum_ref, ds_ref, *, seqs, taps,
):
    rows, width = c_ref.shape
    halo = r_ref.shape[0] - rows
    count = rows // seqs
    si, sd, conv = si_ref[...], sd_ref[...], c_ref[...]
    rate = v_ref[taps + 3 : taps + 4, :]
    decay = jnp.exp(sd * rate)
    at_start = start_rows(first_ref, rows, seqs, width)
    scale, spare = input_scale(decay, at_start)
    grad = late_ref[...]
    for p in range(count - 1, -1, -1):
        grad = t_ref[pl.ds(p * seqs, seqs), :] + grad
        ds_ref[pl.ds(p * seqs, seqs), :] = grad
        grad = decay[p * seqs : (p + 1) * seqs] * grad
    ds = ds_ref[...]
    before = carry_ref[...] if count == 1 else jnp.concatenate([carry_ref[...], s_ref[pl.ds(0, rows - seqs), :]], axis=0)
    bends = jnp.logical_and(spare > 0.001, jnp.logical_not(at_start))
    d_scale = jnp.where(bends, -(decay * decay) / scale, 0.0)
    gated = ds * conv
    d_log = ds * before * decay + gated * si * d_scale
    d_in = (gated * scale * si * (1.0 - si)).astype(BF16)
    d_dec = (d_log * rate * sd * (1.0 - sd)).astype(BF16)
    low = conv.astype(BF16)
    gi_ref[...] = dot(low, d_in, ((0,), (0,))).astype(gi_ref.dtype)
    gd_ref[...] = dot(low, d_dec, ((0,), (0,))).astype(gd_ref.dtype)
    dc = ds * si * scale + dot(d_in, wi_ref[...], ((1,), (1,))) + dot(d_dec, wd_ref[...], ((1,), (1,)))
    dc_ref[...] = dc

    def total(values):
        return jnp.sum(values, axis=0, keepdims=True)

    parts = [
        total(d_in.astype(F32)),
        total(d_dec.astype(F32)),
        total(d_log * sd) * v_ref[taps + 4 : taps + 5, :],
        total(dc),
    ]
    for k in range(taps):
        parts.append(total(r_ref[pl.ds(halo - k * seqs, rows), :] * dc))
    sum_ref[...] = jnp.concatenate(parts, axis=0)


def head_calls(heads, width, rows, halo_rows, seqs, taps):
    def cols(n):
        return pl.BlockSpec((n, width), lambda h: (0, h))

    flag = pl.BlockSpec(memory_space=pltpu.SMEM)
    full = heads * width
    params = pltpu.CompilerParams(vmem_limit_bytes=48 * 1024 * 1024)
    vec_rows = 16

    def shape(n, kind=F32):
        return jax.ShapeDtypeStruct((n, full), kind)

    def call(kernel, ins, outs, shapes, scratch=(), flops=0):
        return pl.pallas_call(
            functools.partial(kernel, seqs=seqs, taps=taps),
            grid=(heads,),
            in_specs=ins,
            out_specs=outs,
            out_shape=shapes,
            scratch_shapes=list(scratch),
            compiler_params=params,
            cost_estimate=SMALL,
        )

    unit = 2 * rows * full * width
    return (
        call(
            gates_kernel,
            [flag, cols(halo_rows), cols(vec_rows), cols(width), cols(width)],
            [cols(rows), cols(rows), cols(rows), cols(seqs), cols(seqs)],
            [shape(rows), shape(rows), shape(rows), shape(seqs), shape(seqs)],
            flops=2 * unit,
        ),
        call(
            states_kernel,
            [flag, cols(rows), cols(rows), cols(rows), cols(rows), cols(vec_rows), cols(seqs)],
            [cols(rows), cols(rows)],
            [shape(rows), shape(rows, BF16)],
        ),
        call(
            branch_kernel,
            [cols(rows), cols(rows), cols(rows), cols(rows), cols(vec_rows)],
            [cols(rows), cols(rows), cols(seqs), cols(8)],
            [shape(rows), shape(rows, BF16), shape(seqs), shape(8)],
        ),
        call(
            core_kernel,
            [flag, cols(rows), cols(rows), cols(rows), cols(rows), cols(rows), cols(halo_rows), cols(vec_rows),
             cols(seqs), cols(seqs), cols(width), cols(width)],
            [cols(rows), cols(width), cols(width), cols(4 + taps)],
            [shape(rows), shape(width, BF16), shape(width, BF16), shape(4 + taps)],
            scratch=[pltpu.VMEM((rows, width), F32)],
            flops=4 * unit,
        ),
    )


def row_tile(rows):
    return max(n for n in (512, 256, 128, 64, 32, 16) if rows % n == 0)


def feed_kernel(at_ref, x_ref, d_ref, w_ref, b_ref, h_ref, g_ref, *, first_unit):
    step = h_ref.shape[1]
    pre = dot(x_ref[...], w_ref[:, : 2 * step]) + b_ref[...]
    d_hidden = dot(d_ref[...], w_ref[:, 2 * step :])
    gate, up = pre[:, :step], pre[:, step:]
    mine = lax.broadcasted_iota(jnp.int32, gate.shape, 1) + first_unit < at_ref[0]
    value, slope = gelu_parts(gate)
    h_ref[...] = jnp.where(mine, value * up, 0.0).astype(BF16)
    g_ref[:, :step] = jnp.where(mine, d_hidden * up * slope, 0.0).astype(BF16)
    g_ref[:, step:] = jnp.where(mine, d_hidden * value, 0.0).astype(BF16)


def feed(owned, x, d, weights, bias, first_unit):
    rows, width = x.shape
    step = weights.shape[1] // 3
    tile = row_tile(rows)
    return pl.pallas_call(
        functools.partial(feed_kernel, first_unit=first_unit),
        grid=(rows // tile,),
        in_specs=[
            pl.BlockSpec(memory_space=pltpu.SMEM),
            pl.BlockSpec((tile, width), lambda i: (i, 0)),
            pl.BlockSpec((tile, width), lambda i: (i, 0)),
            pl.BlockSpec((width, 3 * step), lambda i: (0, 0)),
            pl.BlockSpec((1, 2 * step), lambda i: (0, 0)),
        ],
        out_specs=[
            pl.BlockSpec((tile, step), lambda i: (i, 0)),
            pl.BlockSpec((tile, 2 * step), lambda i: (i, 0)),
        ],
        out_shape=[
            jax.ShapeDtypeStruct((rows, step), BF16),
            jax.ShapeDtypeStruct((rows, 2 * step), BF16),
        ],
        compiler_params=pltpu.CompilerParams(vmem_limit_bytes=VMEM_BYTES),
        cost_estimate=SMALL,
    )(owned, x, d, weights, bias)


def grad_kernel(x_ref, d_ref, g_ref, h_ref, o_ref, sum_ref):
    step = h_ref.shape[1]

    @pl.when(pl.program_id(0) == 0)
    def _():
        total = jnp.sum(g_ref[...].astype(F32), axis=0, keepdims=True)
        sum_ref[...] = jnp.broadcast_to(total, sum_ref.shape)

    o_ref[:, : 2 * step] = dot(x_ref[...], g_ref[...], ((0,), (0,))).astype(BF16)
    o_ref[:, 2 * step :] = dot(d_ref[...], h_ref[...], ((0,), (0,))).astype(BF16)


def feed_grads(x, d, d_pre, hidden):
    rows, width = x.shape
    step = hidden.shape[1]
    tile = 512 if width % 512 == 0 else width
    return pl.pallas_call(
        grad_kernel,
        grid=(width // tile,),
        in_specs=[
            pl.BlockSpec((rows, tile), lambda i: (0, i)),
            pl.BlockSpec((rows, tile), lambda i: (0, i)),
            pl.BlockSpec((rows, 2 * step), lambda i: (0, 0)),
            pl.BlockSpec((rows, step), lambda i: (0, 0)),
        ],
        out_specs=[pl.BlockSpec((tile, 3 * step), lambda i: (i, 0)), pl.BlockSpec((8, 2 * step), lambda i: (0, 0))],
        out_shape=[jax.ShapeDtypeStruct((width, 3 * step), BF16), jax.ShapeDtypeStruct((8, 2 * step), F32)],
        compiler_params=pltpu.CompilerParams(vmem_limit_bytes=VMEM_BYTES),
        cost_estimate=SMALL,
    )(x, d, d_pre, hidden)


def back_kernel(*refs):
    count = (len(refs) - 1) // 2
    out = dot(refs[0][...], refs[count][...], ((1,), (1,)))
    for k in range(1, count):
        out = out + dot(refs[k][...], refs[count + k][...], ((1,), (1,)))
    refs[-1][...] = out.astype(BF16)


def feed_back(values, weights, part, block, blocks):
    rows, cols = values[0].shape
    rows = rows // blocks
    width = weights[0].shape[0]
    tile = 512 if width % 512 == 0 else width
    return pl.pallas_call(
        back_kernel,
        grid=(width // tile,),
        in_specs=[pl.BlockSpec((rows, cols), lambda i: (part, 0)) for _ in values]
        + [pl.BlockSpec((tile, cols), lambda i: (i, block)) for _ in weights],
        out_specs=pl.BlockSpec((rows, tile), lambda i: (0, i)),
        out_shape=jax.ShapeDtypeStruct((rows, width), BF16),
        compiler_params=pltpu.CompilerParams(vmem_limit_bytes=VMEM_BYTES),
        cost_estimate=SMALL,
    )(*values, *weights)


def swap(v, axis):
    return lax.ppermute(v, axis, [(0, 1), (1, 0)])


def gather_rows(v, axis):
    if lax.axis_size(axis) == 2:
        return jnp.concatenate([v, swap(v, axis)], axis=0)
    return lax.all_gather(v, axis, axis=0, tiled=True)


def scatter_rows(v, axis):
    if lax.axis_size(axis) == 2:
        half = v.shape[0] // 2
        return (v[:half].astype(F32) + swap(v[half:], axis).astype(F32)).astype(BF16)
    return lax.psum_scatter(v, axis, scatter_dimension=0, tiled=True)


def gather_plane(v):
    if lax.axis_size("x") != 2:
        return gather_rows(gather_rows(v, "x"), "y")
    half = v.shape[0] // 2
    a, b = v[:half], v[half:]
    ax, by = swap(a, "x"), swap(b, "y")
    a, b = jnp.concatenate([a, ax], axis=0), jnp.concatenate([b, by], axis=0)
    return jnp.concatenate([a, swap(a, "y"), b, swap(b, "x")], axis=0)


def replicated_plane(own, side):
    if lax.axis_size("x") != 2:
        return gather_plane(own)
    half = own.shape[0] // 2
    near = swap(own, "x")
    far = swap(near, "y")
    return jnp.concatenate(
        [own[:half], near[:half], side[:half], far[:half], own[half:], side[half:], near[half:], far[half:]], axis=0
    )


def scatter_plane(v, *beside):
    if lax.axis_size("x") != 2:
        return (scatter_rows(scatter_rows(v, "y"), "x").astype(F32), *beside)
    half = v.shape[0] // 2
    quarter = half // 2
    a = v[:half].reshape(2, 2, quarter // 2, -1).swapaxes(0, 1).reshape(half, -1)
    b = v[half:].reshape(2, 2, quarter // 2, -1).swapaxes(0, 1).reshape(half, -1)
    got_a, got_b, *beside = tie(swap(a[quarter:], "x"), swap(b[quarter:], "y"), *beside)

    def fold(rows, got):
        return rows.astype(F32) + got.astype(F32)

    a, b = fold(a[:quarter], got_a).astype(BF16), fold(b[:quarter], got_b).astype(BF16)
    keep = quarter // 2
    a, b = fold(a[:keep], swap(a[keep:], "y")), fold(b[:keep], swap(b[keep:], "x"))
    return (jnp.concatenate([a, b], axis=0), *beside)


def scatter_side(v):
    if lax.axis_size("x") != 2:
        return scatter_rows(v, "y")
    count = v.shape[0] // 8
    a, b = v[: 4 * count].reshape(4, count, -1), v[4 * count :].reshape(4, count, -1)
    keep = jnp.concatenate([a[0], b[0], a[1], b[2]], axis=0)
    send = jnp.concatenate([a[2], b[1], a[3], b[3]], axis=0)
    return keep, swap(send, "y")


def gather_group(v):
    return gather_rows(gather_rows(v, "x"), "c")


def deal_group(v):
    mid, count = lax.axis_size("x"), v.shape[1]
    v = v.reshape(PLANES, mid * CORES, -1, count)
    if mid != 2:
        got = lax.all_gather(v, "x", axis=3, tiled=True)
        got = gather_cols(got)
        return lax.dynamic_index_in_dim(got, lax.axis_index(("x", "c")), 1, keepdims=False).reshape(-1, got.shape[-1])
    me = lax.axis_index(("x", "c"))
    parts = []
    for flip in (0, 2, 1, 3):
        part = lax.dynamic_index_in_dim(v, jnp.bitwise_xor(me, flip), 1, keepdims=False)
        parts.append(lax.ppermute(part, ("x", "c"), [(j, j ^ flip) for j in range(4)]) if flip else part)
    return jnp.concatenate(parts, axis=-1).reshape(-1, 4 * count)


def gather_cols(v):
    return jnp.concatenate([v, swap(v, "c")], axis=-1)


def fold_cores(v):
    v = v.reshape(lax.axis_size("z"), lax.axis_size("x"), CORES, *v.shape[1:])
    at = lax.axis_index("c")
    own = lax.dynamic_index_in_dim(v, at, 2, keepdims=False)
    return (own.astype(F32) + swap(lax.dynamic_index_in_dim(v, 1 - at, 2, keepdims=False), "c").astype(F32)).astype(BF16)


def fold_mid(v):
    if lax.axis_size("x") != 2:
        return lax.psum_scatter(v, "x", scatter_dimension=1, tiled=False)
    at = lax.axis_index("x")
    own = lax.dynamic_index_in_dim(v, at, 1, keepdims=False)
    return (own.astype(F32) + swap(lax.dynamic_index_in_dim(v, 1 - at, 1, keepdims=False), "x").astype(F32)).astype(BF16)


def fold_planes(v):
    return lax.psum_scatter(v, "z", scatter_dimension=0, tiled=False).astype(F32)


def sum_plane(v):
    v = v + swap(v, "c")
    return v + swap(v, "x") if lax.axis_size("x") == 2 else lax.psum(v, "x")


def sum_planes(v):
    count = lax.axis_size("z")
    return sum([lax.ppermute(v, "z", [(j, (j + far) % count) for j in range(count)]) for far in range(1, count)], v)


def to_slices(v):
    if lax.axis_size("x") != 2:
        return lax.all_to_all(v, ("x", "c"), split_axis=0, concat_axis=0, tiled=True)
    me = lax.axis_index(("x", "c"))
    pick = functools.partial(lax.dynamic_slice_in_dim, slice_size=1, axis=0)
    out = lax.dynamic_update_slice_in_dim(jnp.zeros_like(v), pick(v, me), me, 0)
    for flip in (1, 2, 3):
        other = jnp.bitwise_xor(me, flip)
        got = lax.ppermute(pick(v, other), ("x", "c"), [(j, j ^ flip) for j in range(4)])
        out = lax.dynamic_update_slice_in_dim(out, got, other, 0)
    return out


def halves(v, axis):
    half = v.shape[0] // 2
    at = lax.axis_index(axis)
    own = lax.dynamic_slice_in_dim(v, at * half, half, 0)
    return own, lax.dynamic_slice_in_dim(v, (1 - at) * half, half, 0)


def whole_rows(own, axis):
    other = swap(own, axis)
    low = lax.axis_index(axis) == 0
    return jnp.concatenate([jnp.where(low, own, other), jnp.where(low, other, own)], axis=0)


def ranks(value, axis):
    count = lax.axis_size(axis)
    if count == 2:
        other = swap(value, axis)
        low = lax.axis_index(axis) == 0
        return [jnp.where(low, value, other), jnp.where(low, other, value)]
    every = lax.all_gather(value, axis)
    return [every[j] for j in range(count)]


def carry_in(state, total, backward):
    pair = jnp.stack([state, total])
    inner = []
    for axis, kind in (("c", F32), ("x", BF16)):
        parts = [part.astype(F32) for part in ranks(pair.astype(kind), axis)]
        order = range(len(parts))
        at = lax.axis_index(axis)
        if backward:
            order, at = [len(parts) - 1 - j for j in order], len(parts) - 1 - at
        gone = jnp.stack([jnp.zeros_like(state), jnp.ones_like(total)])
        mine = gone
        for place, j in enumerate(order):
            mine = jnp.where(at == place, gone, mine)
            gone = jnp.stack([parts[j][0] + parts[j][1] * gone[0], parts[j][1] * gone[1]])
        inner.append(mine)
        pair = gone
    planes = lax.axis_size("z")
    sent = pair.astype(BF16)
    entering = jnp.zeros_like(state)
    steps = []
    for far in range(1, planes):
        if backward:
            route = [(j + far, j) for j in range(planes - far)]
        else:
            route = [(j, j + far) for j in range(planes - far)]
        steps.append(lax.ppermute(sent if far < planes - 1 else sent[:1], "z", route).astype(F32))
    for step in reversed(steps):
        entering = step[0] + (step[1] * entering if step.shape[0] == 2 else 0.0)
    for mine in reversed(inner):
        entering = mine[0] + mine[1] * entering
    return entering


def norm(v, gain):
    scale = lax.rsqrt(jnp.mean(v * v, axis=-1, keepdims=True) + 1e-6)
    return v * scale * gain, scale


def norm_back(v, scale, gain, d_out):
    scaled = gain * d_out
    mean = jnp.mean(v * scaled, axis=-1, keepdims=True)
    return scale * scaled - v * (scale * scale * scale * mean), jnp.sum(v * scale * d_out, axis=0)


def body(
    block_input, cotangent, seq_lengths, pre_gain, w_branch, b_branch, w_recur, b_recur, conv_kernel, conv_bias,
    input_gate_weight, input_gate_bias, decay_gate_weight, decay_gate_bias, decay_base, w_output, b_output,
    ffn_gain, w_expand, b_expand, w_shrink, b_shrink,
):
    mid = lax.axis_size("x")
    groups = PLANES * mid * CORES
    place = lax.axis_index(DP)
    side = lax.axis_index("y")
    seqs, pieces, width = block_input.shape
    rows = seqs * pieces
    taps, heads, head_part = conv_kernel.shape
    head_size = head_part * groups
    channels = heads * head_size
    part = w_recur.shape[0]
    units = w_shrink.shape[1]
    halo = (taps - 1) * seqs

    x_low = block_input.transpose(1, 0, 2).reshape(rows, width)
    positions = place * pieces + lax.broadcasted_iota(jnp.int32, (pieces, seqs), 0)
    mask = (positions < seq_lengths[None, :]).reshape(rows, 1)
    d_out = jnp.where(mask, cotangent.transpose(1, 0, 2).reshape(rows, width), 0).astype(BF16)
    early = lax.ppermute(x_low[rows - halo :], DP, [(j, j + 1) for j in range(groups - 1)])

    recur_stack = lax.all_gather(jnp.stack([w_recur, w_branch, w_output]), DP, axis=1, tiled=True)
    inlet_full = lax.all_gather(input_gate_weight.transpose(1, 0, 2).reshape(head_part, channels), DP, axis=0, tiled=True)
    decay_full = lax.all_gather(decay_gate_weight.transpose(1, 0, 2).reshape(head_part, channels), DP, axis=0, tiled=True)
    vectors = jnp.stack([b_branch, b_recur, *[conv_kernel[k] for k in range(taps)], conv_bias, input_gate_bias,
                         decay_gate_bias, decay_base])
    flat = jnp.concatenate([vectors.reshape(-1), pre_gain, b_output, ffn_gain, b_shrink, b_expand.reshape(-1)])
    every = lax.all_gather(flat, DP, axis=0, tiled=False).astype(F32)
    taken = 0

    def take(count):
        nonlocal taken
        taken += count
        return every[:, taken - count : taken]

    by_head = take(vectors.size).reshape(groups, -1, head_part).transpose(1, 0, 2).reshape(-1, channels)
    vec_branch, vec_recur, vec_taps = by_head[0], by_head[1], by_head[2 : 2 + taps]
    vec_base = by_head[5 + taps]
    gain_one, vec_output, gain_two, vec_shrink = [take(part).reshape(width) for _ in range(4)]
    blocks = b_expand.shape[1]
    vec_expand = take(2 * blocks * head_part).reshape(groups, 2, blocks, head_part).transpose(1, 2, 0, 3).reshape(2, units)
    gain_one, gain_two = 1.0 + gain_one, 1.0 + gain_two
    rates = jnp.stack([-8.0 * jax.nn.softplus(vec_base), -8.0 * jax.nn.sigmoid(vec_base)])
    coefs = jnp.concatenate([by_head[2 : 5 + taps], rates], axis=0)
    coefs = jnp.pad(coefs, ((0, 16 - coefs.shape[0]), (0, 0)))

    first = (place == 0).astype(jnp.int32).reshape(1)
    x_ext = jnp.concatenate([early, x_low], axis=0).astype(F32)
    normed_f, _ = norm(x_ext, gain_one)
    normed_ext = normed_f.astype(BF16)
    d_own, d_side = halves(d_out, "y")

    slices = mid * CORES
    tiles = units // LANES
    wide_tiles = -(-tiles // slices)
    wide = wide_tiles * LANES
    starts = [j * (tiles - wide_tiles) // (slices - 1) for j in range(slices)]
    owned = [(starts[j + 1] if j + 1 < slices else tiles) - starts[j] for j in range(slices)]
    chunks = CHUNKS if wide % (CHUNKS * LANES) == 0 else 1
    step = wide // chunks
    sent = []
    for j in range(slices):
        for k in range(chunks):
            at = starts[j] * LANES + k * step
            sent += [w_expand[0, :, at : at + step], w_expand[1, :, at : at + step], w_shrink[:, at : at + step]]
    per = 3 * chunks

    def to_send(low, high):
        mine = [jnp.concatenate(sent[j * per + 3 * k : j * per + 3 * k + 3], axis=1) for j in range(slices) for k in range(low, high)]
        return jnp.stack(mine).reshape(slices, high - low, part, 3 * step)

    def to_plane(mine):
        got = to_slices(mine)
        return [got[:, k].reshape(slices * part, 3 * step) for k in range(got.shape[1])]

    early_chunks = 1
    held = to_plane(to_send(0, early_chunks))
    later = to_send(early_chunks, chunks) if early_chunks < chunks else held[0]
    my_slice = lax.axis_index(("x", "c"))
    my_start = jnp.array(starts, jnp.int32)[my_slice] * LANES
    my_owned = jnp.array(owned, jnp.int32)[my_slice] * LANES
    my_bias = lax.dynamic_slice_in_dim(vec_expand, my_start, wide, 1)
    recur_stack, normed_ext, coefs, inlet_full, decay_full, my_bias, d_out, d_own, d_side, later, *held = tie(
        recur_stack, normed_ext, coefs, inlet_full, decay_full, my_bias, d_out, d_own, d_side, later, *held
    )
    recur_full, branch_full, output_full = recur_stack[0], recur_stack[1], recur_stack[2]
    if early_chunks < chunks:
        held += to_plane(later)
    ffn_full = [lax.all_gather(weights, "z", axis=0, tiled=True) for weights in held]

    d_plane = gather_rows(replicated_plane(d_own, d_side), "c")

    gates, states, branch_back, core_back = head_calls(heads, head_size, rows, rows + halo, seqs, taps)
    normed = normed_ext[halo:]
    recur = dot(normed_ext, recur_full) + vec_recur
    ext_row = lax.broadcasted_iota(jnp.int32, (rows + halo, 1), 0)
    recur = jnp.where(jnp.logical_and(ext_row < halo, place == 0), 0.0, recur)
    conv, sig_in, sig_dec, end, total = gates(first, recur, coefs, inlet_full, decay_full)
    carry = carry_in(end, total, False)
    branch = dot(normed, branch_full) + vec_branch
    state, mixed = states(first, conv, sig_in, sig_dec, branch, coefs, carry)
    mixed_own, mixed_other = halves(mixed, "y")
    out_other = dot(mixed_other, output_full, ((1,), (1,))).astype(BF16)
    got = swap(out_other, "y")
    out_own = dot(mixed_own, output_full, ((1,), (1,)))
    x_own, _ = halves(x_low, "y")
    x_own = x_own.astype(F32)
    middle = x_own + out_own + got.astype(F32) + vec_output
    second_f, scale_two = norm(middle, gain_two)
    second = second_f.astype(BF16)

    pair = gather_plane(second)
    plane = gather_rows(pair, "c")
    hidden, d_pre, ffn_grads, bias_grads = [], [], [], []
    owned_units = my_owned.reshape(1)
    mixed, normed, plane = tie(mixed, normed, plane)
    normed_dealt, mixed_group = deal_group(normed.T), gather_group(mixed)
    for k in range(chunks):
        bias = my_bias[:, k * step : (k + 1) * step].reshape(1, 2 * step)
        if k == chunks - 1:
            ffn_full[k], normed_dealt, mixed_group, *bias_grads = tie(ffn_full[k], normed_dealt, mixed_group, *bias_grads)
        hid, pre = feed(owned_units, plane, d_plane, ffn_full[k], bias, k * step)
        hidden.append(hid)
        d_pre.append(pre)
        if k + 1 < chunks:
            grads, sums = feed_grads(plane, d_plane, pre, hid)
            ffn_grads.append(grads)
            bias_grads.append(sums)

    def pair_sum(values, block):
        other = feed_back(values, ffn_full, 1, block, CORES)
        own = feed_back(values, ffn_full, 0, block, CORES)
        arrived, own = tie(swap(other, "c"), own)
        return (own.astype(F32) + arrived.astype(F32)).astype(BF16)

    d_pair = pair_sum(d_pre, 0)
    d_pair, *hidden = tie(d_pair, *hidden)
    last_grads, last_sums = feed_grads(plane, d_plane, d_pre[-1], hidden[-1])
    d_second_own, last_sums = scatter_plane(d_pair, last_sums)
    bias_grads = [sums[0].reshape(2, step) for sums in [*bias_grads, last_sums]]
    ffn_grads = [lax.psum_scatter(grad, "z", scatter_dimension=0, tiled=True) for grad in ffn_grads + [last_grads]]
    d_middle, grad_gain_two = norm_back(middle, scale_two, gain_two, d_second_own)
    d_middle = d_middle + d_own.astype(F32)
    d_low_own = d_middle.astype(BF16)
    d_low_own, *hidden = tie(d_low_own, *hidden)
    low_other, out_pair = tie(swap(d_low_own, "y"), pair_sum(hidden, 2))
    out_side = scatter_side(out_pair)
    is_low = side == 0
    d_low = jnp.concatenate([jnp.where(is_low, d_low_own, low_other), jnp.where(is_low, low_other, d_low_own)], axis=0)
    d_mixed = dot(d_low, output_full)
    pulled, d_branch, end_back, branch_sum = branch_back(d_mixed, branch, state, sig_dec, coefs)
    low_dealt = deal_group(d_low.T)
    end_back, low_dealt = tie(end_back, low_dealt)
    late = carry_in(end_back, total, True)

    def by_plane(grad):
        return grad.astype(BF16).reshape(PLANES, part, channels)

    def by_owner(grad):
        return grad.reshape(groups, -1, channels)

    d_normed_first = dot(d_branch, branch_full, ((1,), (1,)))
    late, d_normed_first, *out_side = tie(late, d_normed_first, *(out_side if mid == 2 else [out_side]))
    if mid == 2:
        out_side = ((out_side[0].astype(F32) + out_side[1].astype(F32)).astype(BF16),)
    out_side = out_side[0]
    d_conv, grad_inlet, grad_decay, core_sums = core_back(
        first, pulled, conv, sig_in, sig_dec, state, recur, coefs, carry, late, inlet_full, decay_full
    )
    branch_group = gather_group(d_branch)
    d_conv, branch_group = tie(d_conv, branch_group)
    behind = lax.ppermute(d_conv[:halo].astype(BF16), DP, [(j + 1, j) for j in range(groups - 1)])
    d_ext = jnp.concatenate([d_conv, behind.astype(F32)], axis=0)
    d_recur = vec_taps[0] * d_ext[:rows]
    for k in range(1, taps):
        d_recur = d_recur + vec_taps[k] * d_ext[k * seqs : k * seqs + rows]
    d_recur = d_recur.astype(BF16)
    recur_near = swap(d_recur, "x") if mid == 2 else lax.all_gather(d_recur, "x", axis=0, tiled=True)
    gates_b = fold_mid(fold_cores(jnp.concatenate([by_owner(grad_inlet), by_owner(grad_decay)], axis=1)))
    grad_output, grad_branch = dot(low_dealt, mixed_group), dot(normed_dealt, branch_group)
    packed = [by_plane(grad_output), by_plane(grad_branch)]
    recur_near, gates_b, *packed = tie(recur_near, gates_b, *packed)
    recur_near = jnp.concatenate([d_recur, recur_near], axis=0) if mid == 2 else recur_near
    packed += [by_plane(dot(normed_dealt, gather_rows(recur_near, "c"))), gates_b]
    packed = jnp.concatenate(packed, axis=1)
    packed, d_recur = tie(packed, d_recur)
    d_normed = d_normed_first + dot(d_recur, recur_full, ((1,), (1,)))
    dn_own, dn_other = halves(d_normed, "y")
    dn_got = swap(dn_other.astype(BF16), "y")
    packed, dn_got, out_side, *ffn_grads = tie(packed, dn_got, out_side, *ffn_grads)
    sums = fold_planes(packed)
    dn_own = dn_own + dn_got.astype(F32)
    scale_one = lax.rsqrt(jnp.mean(x_own * x_own, axis=-1, keepdims=True) + 1e-6)
    d_input, grad_gain_one = norm_back(x_own, scale_one, gain_one, dn_own)
    d_input = whole_rows((d_middle + d_input).astype(BF16), "y")

    shared = jnp.stack([grad_gain_one, jnp.sum(d_low_own.astype(F32), axis=0), grad_gain_two])
    shared = shared + swap(shared, "y")
    recur_sum = jnp.sum(d_recur.astype(F32), axis=0)
    by_unit = lax.dynamic_update_slice_in_dim(jnp.zeros((2, units), F32), jnp.concatenate(bias_grads, axis=1), my_start, 1)
    small = jnp.concatenate(
        [
            jnp.concatenate([branch_sum[:1], recur_sum[None], core_sums[4:], core_sums[3:4], core_sums[:3]], axis=0),
            shared.reshape(-1, channels),
            jnp.sum(d_out.astype(F32), axis=0).reshape(-1, channels),
            by_unit.reshape(-1, channels),
        ],
        axis=0,
    )
    small = sum_plane(small)
    returned = jnp.stack([grad.reshape(slices, part, 3 * step) for grad in ffn_grads], axis=1)
    small, out_side, returned = tie(small, out_side, returned)

    mask_own, _ = halves(mask, "y")
    result = jnp.where(mask_own, middle + scatter_rows(out_side, "x").astype(F32) + vec_shrink, 0.0).astype(BF16)
    result = whole_rows(result, "y")
    small = sum_planes(small)
    count = 6 + taps
    head_sums = lax.dynamic_slice_in_dim(small[:count].reshape(count, heads, head_size), place * head_part, head_part, 2)
    features = 4 * (width // channels)
    feature_sums = lax.dynamic_slice_in_dim(small[count : count + features].reshape(4, width), place * part, part, 1)
    unit_sums = small[count + features :].reshape(2, blocks, head_size)
    g_b_expand = lax.dynamic_slice_in_dim(unit_sums, place * head_part, head_part, 2)
    g_b_branch, g_b_recur, g_kernel = head_sums[0], head_sums[1], head_sums[2 : 2 + taps]
    g_conv_bias, g_b_inlet, g_b_decay, g_base = [head_sums[2 + taps + j] for j in range(4)]
    g_pre_gain, g_b_output, g_ffn_gain, g_b_shrink = [feature_sums[j] for j in range(4)]

    ffn_sum = to_slices(returned)
    grads_out = []
    for kind in range(3):
        pieces_out = []
        for j in range(slices):
            for k in range(chunks):
                keep = min(step, owned[j] * LANES - k * step)
                if keep > 0:
                    pieces_out.append(ffn_sum[j, k, :, kind * step : kind * step + keep])
        grads_out.append(jnp.concatenate(pieces_out, axis=1).astype(F32))
    grad_expand = jnp.stack(grads_out[:2])
    grad_shrink = grads_out[2]

    def gate_out(at):
        return sums[at : at + head_part].reshape(head_part, heads, head_size).transpose(1, 0, 2)

    def rows_out(v):
        return v.reshape(pieces, seqs, width).transpose(1, 0, 2)

    return (
        rows_out(result), rows_out(d_input), g_pre_gain, sums[part : 2 * part], g_b_branch, sums[2 * part : 3 * part], g_b_recur,
        g_kernel, g_conv_bias, gate_out(3 * part), g_b_inlet, gate_out(3 * part + head_part), g_b_decay, g_base,
        sums[:part], g_b_output, g_ffn_gain, grad_expand, g_b_expand, grad_shrink, g_b_shrink,
    )


def solution(mesh):
    groups, sides = mesh.shape["dp"], mesh.shape["tensor"]
    mid = groups // (PLANES * CORES)
    grid = Mesh(mesh.devices.reshape(PLANES, mid, CORES, sides), ("z", "x", "c", "y"))
    rows, vec = P(None, DP, None), P(DP)
    mat, head, tap, gate = P(DP, "y"), P("y", DP), P(None, "y", DP), P("y", DP, None)
    wide = P(None, DP, "y")
    return jax.shard_map(
        body,
        mesh=grid,
        in_specs=(
            rows, rows, P(), vec, mat, head, mat, head, tap, head, gate, head, gate, head, head, mat, vec, vec,
            wide, tap, mat, vec,
        ),
        out_specs=(
            rows, rows, vec, mat, head, mat, head, tap, head, gate, head, gate, head, head, mat, vec, vec,
            wide, tap, mat, vec,
        ),
        check_vma=False,
    )
```

```python
import functools

import jax
import jax.numpy as jnp
from jax import lax
from jax.experimental import pallas as pl
from jax.experimental.pallas import tpu as pltpu
from jax.sharding import Mesh, PartitionSpec as P

F32, BF16 = jnp.float32, jnp.bfloat16
LANES = 128
PLANES = 4
CORES = 2
CHUNKS = 2
VMEM_BYTES = 56 * 1024 * 1024
SMALL = pl.CostEstimate(flops=1, bytes_accessed=1, transcendentals=0)
DP = ("z", "x", "c")
GELU_A, GELU_B = 0.7978845608028654, 0.044715


def gelu_parts(v):
    square = v * v
    bent = jnp.tanh(GELU_A * v * (1.0 + GELU_B * square))
    half = 0.5 * (1.0 + bent)
    slope = half + 0.5 * v * (1.0 - bent * bent) * (GELU_A * (1.0 + 3.0 * GELU_B * square))
    return v * half, slope


def gelu(v):
    return v * (0.5 * (1.0 + jnp.tanh(GELU_A * v * (1.0 + GELU_B * v * v))))


def dot(a, b, dims=((1,), (0,))):
    return lax.dot_general(a, b, (dims, ((), ())), preferred_element_type=F32)


def tie(*values):
    return lax.optimization_barrier(values)


def input_scale(decay, at_start):
    spare = 1.0 - decay * decay
    scale = jnp.sqrt(jnp.maximum(spare, 0.001))
    return jnp.where(at_start, 1.0, scale), spare


def start_rows(first_ref, rows, seqs, width):
    row = lax.broadcasted_iota(jnp.int32, (rows, width), 0)
    return jnp.logical_and(row < seqs, first_ref[0] == 1)


def gates_kernel(first_ref, r_ref, v_ref, wi_ref, wd_ref, c_ref, si_ref, sd_ref, e_ref, p_ref, *, seqs, taps):
    rows, width = c_ref.shape
    halo = r_ref.shape[0] - rows
    conv = v_ref[taps : taps + 1, :] + v_ref[0:1, :] * r_ref[pl.ds(halo, rows), :]
    for k in range(1, taps):
        conv = conv + v_ref[k : k + 1, :] * r_ref[pl.ds(halo - k * seqs, rows), :]
    c_ref[...] = conv
    low = conv.astype(BF16)
    si = jax.nn.sigmoid(dot(low, wi_ref[...]) + v_ref[taps + 1 : taps + 2, :])
    sd = jax.nn.sigmoid(dot(low, wd_ref[...]) + v_ref[taps + 2 : taps + 3, :])
    si_ref[...] = si
    sd_ref[...] = sd
    decay = jnp.exp(sd * v_ref[taps + 3 : taps + 4, :])
    scale, _ = input_scale(decay, start_rows(first_ref, rows, seqs, width))
    source = conv * si * scale
    state, total = source[:seqs], decay[:seqs]
    for p in range(1, rows // seqs):
        a = decay[p * seqs : (p + 1) * seqs]
        state = a * state + source[p * seqs : (p + 1) * seqs]
        total = total * a
    e_ref[...] = state
    p_ref[...] = total


def states_kernel(first_ref, c_ref, si_ref, sd_ref, b_ref, v_ref, carry_ref, s_ref, m_ref, *, seqs, taps):
    rows, width = c_ref.shape
    decay = jnp.exp(sd_ref[...] * v_ref[taps + 3 : taps + 4, :])
    scale, _ = input_scale(decay, start_rows(first_ref, rows, seqs, width))
    source = c_ref[...] * si_ref[...] * scale
    state = carry_ref[...]
    for p in range(rows // seqs):
        at = slice(p * seqs, (p + 1) * seqs)
        state = decay[at] * state + source[at]
        s_ref[pl.ds(p * seqs, seqs), :] = state
    m_ref[...] = (gelu(b_ref[...]) * s_ref[...]).astype(BF16)


def branch_kernel(dm_ref, b_ref, s_ref, sd_ref, v_ref, t_ref, db_ref, e_ref, sum_ref, *, seqs, taps):
    rows, _ = t_ref.shape
    value, slope = gelu_parts(b_ref[...])
    dm = dm_ref[...]
    t = dm * value
    t_ref[...] = t
    db = (dm * s_ref[...] * slope).astype(BF16)
    db_ref[...] = db
    sum_ref[...] = jnp.broadcast_to(jnp.sum(db.astype(F32), axis=0, keepdims=True), sum_ref.shape)
    decay = jnp.exp(sd_ref[...] * v_ref[taps + 3 : taps + 4, :])
    count = rows // seqs
    grad = t[(count - 1) * seqs :]
    for p in range(count - 2, -1, -1):
        grad = t[p * seqs : (p + 1) * seqs] + decay[(p + 1) * seqs : (p + 2) * seqs] * grad
    e_ref[...] = decay[:seqs] * grad


def core_kernel(
    first_ref, t_ref, c_ref, si_ref, sd_ref, s_ref, r_ref, v_ref, carry_ref, late_ref, wi_ref, wd_ref,
    dc_ref, gi_ref, gd_ref, sum_ref, ds_ref, *, seqs, taps,
):
    rows, width = c_ref.shape
    halo = r_ref.shape[0] - rows
    count = rows // seqs
    si, sd, conv = si_ref[...], sd_ref[...], c_ref[...]
    rate = v_ref[taps + 3 : taps + 4, :]
    decay = jnp.exp(sd * rate)
    at_start = start_rows(first_ref, rows, seqs, width)
    scale, spare = input_scale(decay, at_start)
    grad = late_ref[...]
    for p in range(count - 1, -1, -1):
        grad = t_ref[pl.ds(p * seqs, seqs), :] + grad
        ds_ref[pl.ds(p * seqs, seqs), :] = grad
        grad = decay[p * seqs : (p + 1) * seqs] * grad
    ds = ds_ref[...]
    before = carry_ref[...] if count == 1 else jnp.concatenate([carry_ref[...], s_ref[pl.ds(0, rows - seqs), :]], axis=0)
    bends = jnp.logical_and(spare > 0.001, jnp.logical_not(at_start))
    d_scale = jnp.where(bends, -(decay * decay) / scale, 0.0)
    gated = ds * conv
    d_log = ds * before * decay + gated * si * d_scale
    d_in = (gated * scale * si * (1.0 - si)).astype(BF16)
    d_dec = (d_log * rate * sd * (1.0 - sd)).astype(BF16)
    low = conv.astype(BF16)
    gi_ref[...] = dot(low, d_in, ((0,), (0,))).astype(gi_ref.dtype)
    gd_ref[...] = dot(low, d_dec, ((0,), (0,))).astype(gd_ref.dtype)
    dc = ds * si * scale + dot(d_in, wi_ref[...], ((1,), (1,))) + dot(d_dec, wd_ref[...], ((1,), (1,)))
    dc_ref[...] = dc

    def total(values):
        return jnp.sum(values, axis=0, keepdims=True)

    parts = [
        total(d_in.astype(F32)),
        total(d_dec.astype(F32)),
        total(d_log * sd) * v_ref[taps + 4 : taps + 5, :],
        total(dc),
    ]
    for k in range(taps):
        parts.append(total(r_ref[pl.ds(halo - k * seqs, rows), :] * dc))
    sum_ref[...] = jnp.concatenate(parts, axis=0)


def head_calls(heads, width, rows, halo_rows, seqs, taps):
    def cols(n):
        return pl.BlockSpec((n, width), lambda h: (0, h))

    flag = pl.BlockSpec(memory_space=pltpu.SMEM)
    full = heads * width
    params = pltpu.CompilerParams(vmem_limit_bytes=48 * 1024 * 1024)
    vec_rows = 16

    def shape(n, kind=F32):
        return jax.ShapeDtypeStruct((n, full), kind)

    def call(kernel, ins, outs, shapes, scratch=(), flops=0):
        return pl.pallas_call(
            functools.partial(kernel, seqs=seqs, taps=taps),
            grid=(heads,),
            in_specs=ins,
            out_specs=outs,
            out_shape=shapes,
            scratch_shapes=list(scratch),
            compiler_params=params,
            cost_estimate=SMALL,
        )

    unit = 2 * rows * full * width
    return (
        call(
            gates_kernel,
            [flag, cols(halo_rows), cols(vec_rows), cols(width), cols(width)],
            [cols(rows), cols(rows), cols(rows), cols(seqs), cols(seqs)],
            [shape(rows), shape(rows), shape(rows), shape(seqs), shape(seqs)],
            flops=2 * unit,
        ),
        call(
            states_kernel,
            [flag, cols(rows), cols(rows), cols(rows), cols(rows), cols(vec_rows), cols(seqs)],
            [cols(rows), cols(rows)],
            [shape(rows), shape(rows, BF16)],
        ),
        call(
            branch_kernel,
            [cols(rows), cols(rows), cols(rows), cols(rows), cols(vec_rows)],
            [cols(rows), cols(rows), cols(seqs), cols(8)],
            [shape(rows), shape(rows, BF16), shape(seqs), shape(8)],
        ),
        call(
            core_kernel,
            [flag, cols(rows), cols(rows), cols(rows), cols(rows), cols(rows), cols(halo_rows), cols(vec_rows),
             cols(seqs), cols(seqs), cols(width), cols(width)],
            [cols(rows), cols(width), cols(width), cols(4 + taps)],
            [shape(rows), shape(width, BF16), shape(width, BF16), shape(4 + taps)],
            scratch=[pltpu.VMEM((rows, width), F32)],
            flops=4 * unit,
        ),
    )


def row_tile(rows):
    return max(n for n in (512, 256, 128, 64, 32, 16) if rows % n == 0)


def feed_kernel(at_ref, x_ref, d_ref, w_ref, b_ref, h_ref, g_ref, *, first_unit):
    step = h_ref.shape[1]
    pre = dot(x_ref[...], w_ref[:, : 2 * step]) + b_ref[...]
    d_hidden = dot(d_ref[...], w_ref[:, 2 * step :])
    gate, up = pre[:, :step], pre[:, step:]
    mine = lax.broadcasted_iota(jnp.int32, gate.shape, 1) + first_unit < at_ref[0]
    value, slope = gelu_parts(gate)
    h_ref[...] = jnp.where(mine, value * up, 0.0).astype(BF16)
    g_ref[:, :step] = jnp.where(mine, d_hidden * up * slope, 0.0).astype(BF16)
    g_ref[:, step:] = jnp.where(mine, d_hidden * value, 0.0).astype(BF16)


def feed(owned, x, d, weights, bias, first_unit):
    rows, width = x.shape
    step = weights.shape[1] // 3
    tile = row_tile(rows)
    return pl.pallas_call(
        functools.partial(feed_kernel, first_unit=first_unit),
        grid=(rows // tile,),
        in_specs=[
            pl.BlockSpec(memory_space=pltpu.SMEM),
            pl.BlockSpec((tile, width), lambda i: (i, 0)),
            pl.BlockSpec((tile, width), lambda i: (i, 0)),
            pl.BlockSpec((width, 3 * step), lambda i: (0, 0)),
            pl.BlockSpec((1, 2 * step), lambda i: (0, 0)),
        ],
        out_specs=[
            pl.BlockSpec((tile, step), lambda i: (i, 0)),
            pl.BlockSpec((tile, 2 * step), lambda i: (i, 0)),
        ],
        out_shape=[
            jax.ShapeDtypeStruct((rows, step), BF16),
            jax.ShapeDtypeStruct((rows, 2 * step), BF16),
        ],
        compiler_params=pltpu.CompilerParams(vmem_limit_bytes=VMEM_BYTES),
        cost_estimate=SMALL,
    )(owned, x, d, weights, bias)


def grad_kernel(x_ref, d_ref, g_ref, h_ref, o_ref, sum_ref):
    step = h_ref.shape[1]

    @pl.when(pl.program_id(0) == 0)
    def _():
        total = jnp.sum(g_ref[...].astype(F32), axis=0, keepdims=True)
        sum_ref[...] = jnp.broadcast_to(total, sum_ref.shape)

    o_ref[:, : 2 * step] = dot(x_ref[...], g_ref[...], ((0,), (0,))).astype(BF16)
    o_ref[:, 2 * step :] = dot(d_ref[...], h_ref[...], ((0,), (0,))).astype(BF16)


def feed_grads(x, d, d_pre, hidden):
    rows, width = x.shape
    step = hidden.shape[1]
    tile = 512 if width % 512 == 0 else width
    return pl.pallas_call(
        grad_kernel,
        grid=(width // tile,),
        in_specs=[
            pl.BlockSpec((rows, tile), lambda i: (0, i)),
            pl.BlockSpec((rows, tile), lambda i: (0, i)),
            pl.BlockSpec((rows, 2 * step), lambda i: (0, 0)),
            pl.BlockSpec((rows, step), lambda i: (0, 0)),
        ],
        out_specs=[pl.BlockSpec((tile, 3 * step), lambda i: (i, 0)), pl.BlockSpec((8, 2 * step), lambda i: (0, 0))],
        out_shape=[jax.ShapeDtypeStruct((width, 3 * step), BF16), jax.ShapeDtypeStruct((8, 2 * step), F32)],
        compiler_params=pltpu.CompilerParams(vmem_limit_bytes=VMEM_BYTES),
        cost_estimate=SMALL,
    )(x, d, d_pre, hidden)


def back_kernel(*refs):
    count = (len(refs) - 1) // 2
    out = dot(refs[0][...], refs[count][...], ((1,), (1,)))
    for k in range(1, count):
        out = out + dot(refs[k][...], refs[count + k][...], ((1,), (1,)))
    refs[-1][...] = out.astype(BF16)


def feed_back(values, weights, part, block, blocks):
    rows, cols = values[0].shape
    rows = rows // blocks
    width = weights[0].shape[0]
    tile = 512 if width % 512 == 0 else width
    return pl.pallas_call(
        back_kernel,
        grid=(width // tile,),
        in_specs=[pl.BlockSpec((rows, cols), lambda i: (part, 0)) for _ in values]
        + [pl.BlockSpec((tile, cols), lambda i: (i, block)) for _ in weights],
        out_specs=pl.BlockSpec((rows, tile), lambda i: (0, i)),
        out_shape=jax.ShapeDtypeStruct((rows, width), BF16),
        compiler_params=pltpu.CompilerParams(vmem_limit_bytes=VMEM_BYTES),
        cost_estimate=SMALL,
    )(*values, *weights)


def swap(v, axis):
    return lax.ppermute(v, axis, [(0, 1), (1, 0)])


def gather_rows(v, axis):
    if lax.axis_size(axis) == 2:
        return jnp.concatenate([v, swap(v, axis)], axis=0)
    return lax.all_gather(v, axis, axis=0, tiled=True)


def scatter_rows(v, axis):
    if lax.axis_size(axis) == 2:
        half = v.shape[0] // 2
        return (v[:half].astype(F32) + swap(v[half:], axis).astype(F32)).astype(BF16)
    return lax.psum_scatter(v, axis, scatter_dimension=0, tiled=True)


def gather_plane(v):
    if lax.axis_size("x") != 2:
        return gather_rows(gather_rows(v, "x"), "y")
    half = v.shape[0] // 2
    a, b = v[:half], v[half:]
    ax, by = swap(a, "x"), swap(b, "y")
    a, b = jnp.concatenate([a, ax], axis=0), jnp.concatenate([b, by], axis=0)
    return jnp.concatenate([a, swap(a, "y"), b, swap(b, "x")], axis=0)


def replicated_plane(own, side):
    if lax.axis_size("x") != 2:
        return gather_plane(own)
    half = own.shape[0] // 2
    near = swap(own, "x")
    far = swap(near, "y")
    return jnp.concatenate(
        [own[:half], near[:half], side[:half], far[:half], own[half:], side[half:], near[half:], far[half:]], axis=0
    )


def scatter_plane(v, *beside):
    if lax.axis_size("x") != 2:
        return (scatter_rows(scatter_rows(v, "y"), "x").astype(F32), *beside)
    half = v.shape[0] // 2
    quarter = half // 2
    a = v[:half].reshape(2, 2, quarter // 2, -1).swapaxes(0, 1).reshape(half, -1)
    b = v[half:].reshape(2, 2, quarter // 2, -1).swapaxes(0, 1).reshape(half, -1)
    got_a, got_b, *beside = tie(swap(a[quarter:], "x"), swap(b[quarter:], "y"), *beside)

    def fold(rows, got):
        return rows.astype(F32) + got.astype(F32)

    a, b = fold(a[:quarter], got_a).astype(BF16), fold(b[:quarter], got_b).astype(BF16)
    keep = quarter // 2
    a, b = fold(a[:keep], swap(a[keep:], "y")), fold(b[:keep], swap(b[keep:], "x"))
    return (jnp.concatenate([a, b], axis=0), *beside)


def scatter_side(v):
    if lax.axis_size("x") != 2:
        return scatter_rows(v, "y")
    count = v.shape[0] // 8
    a, b = v[: 4 * count].reshape(4, count, -1), v[4 * count :].reshape(4, count, -1)
    keep = jnp.concatenate([a[0], b[0], a[1], b[2]], axis=0)
    send = jnp.concatenate([a[2], b[1], a[3], b[3]], axis=0)
    return keep, swap(send, "y")


def gather_group(v):
    return gather_rows(gather_rows(v, "x"), "c")


def deal_group(v):
    mid, count = lax.axis_size("x"), v.shape[1]
    v = v.reshape(PLANES, mid * CORES, -1, count)
    if mid != 2:
        got = lax.all_gather(v, "x", axis=3, tiled=True)
        got = gather_cols(got)
        return lax.dynamic_index_in_dim(got, lax.axis_index(("x", "c")), 1, keepdims=False).reshape(-1, got.shape[-1])
    me = lax.axis_index(("x", "c"))
    parts = []
    for flip in (0, 2, 1, 3):
        part = lax.dynamic_index_in_dim(v, jnp.bitwise_xor(me, flip), 1, keepdims=False)
        parts.append(lax.ppermute(part, ("x", "c"), [(j, j ^ flip) for j in range(4)]) if flip else part)
    return jnp.concatenate(parts, axis=-1).reshape(-1, 4 * count)


def gather_cols(v):
    return jnp.concatenate([v, swap(v, "c")], axis=-1)


def fold_cores(v):
    v = v.reshape(lax.axis_size("z"), lax.axis_size("x"), CORES, *v.shape[1:])
    at = lax.axis_index("c")
    own = lax.dynamic_index_in_dim(v, at, 2, keepdims=False)
    return (own.astype(F32) + swap(lax.dynamic_index_in_dim(v, 1 - at, 2, keepdims=False), "c").astype(F32)).astype(BF16)


def fold_mid(v):
    if lax.axis_size("x") != 2:
        return lax.psum_scatter(v, "x", scatter_dimension=1, tiled=False)
    at = lax.axis_index("x")
    own = lax.dynamic_index_in_dim(v, at, 1, keepdims=False)
    return (own.astype(F32) + swap(lax.dynamic_index_in_dim(v, 1 - at, 1, keepdims=False), "x").astype(F32)).astype(BF16)


def fold_planes(v):
    return lax.psum_scatter(v, "z", scatter_dimension=0, tiled=False).astype(F32)


def sum_plane(v):
    if lax.axis_size("x") != 2:
        v = v + swap(v, "c")
        return lax.psum(v, "x")
    return sum([lax.ppermute(v, ("x", "c"), [(j, j ^ flip) for j in range(4)]) for flip in (1, 2, 3)], v)


def sum_planes(v):
    count = lax.axis_size("z")
    return sum([lax.ppermute(v, "z", [(j, (j + far) % count) for j in range(count)]) for far in range(1, count)], v)


def sum_line(v):
    return lax.psum_scatter(v, "z", scatter_dimension=0, tiled=True)


def to_slices(v):
    if lax.axis_size("x") != 2:
        return lax.all_to_all(v, ("x", "c"), split_axis=0, concat_axis=0, tiled=True)
    me = lax.axis_index(("x", "c"))
    pick = functools.partial(lax.dynamic_slice_in_dim, slice_size=1, axis=0)
    out = lax.dynamic_update_slice_in_dim(jnp.zeros_like(v), pick(v, me), me, 0)
    for flip in (1, 2, 3):
        other = jnp.bitwise_xor(me, flip)
        got = lax.ppermute(pick(v, other), ("x", "c"), [(j, j ^ flip) for j in range(4)])
        out = lax.dynamic_update_slice_in_dim(out, got, other, 0)
    return out


def halves(v, axis):
    half = v.shape[0] // 2
    at = lax.axis_index(axis)
    own = lax.dynamic_slice_in_dim(v, at * half, half, 0)
    return own, lax.dynamic_slice_in_dim(v, (1 - at) * half, half, 0)


def whole_rows(own, axis):
    other = swap(own, axis)
    low = lax.axis_index(axis) == 0
    return jnp.concatenate([jnp.where(low, own, other), jnp.where(low, other, own)], axis=0)


def ranks(value, axis, beside):
    count = lax.axis_size(axis)
    if count == 2:
        other, *beside = tie(swap(value, axis), *beside)
        low = lax.axis_index(axis) == 0
        return [jnp.where(low, value, other), jnp.where(low, other, value)], beside
    every, *beside = tie(lax.all_gather(value, axis), *beside)
    return [every[j] for j in range(count)], beside


def carry_axis(pair, axis, kind, backward, beside=()):
    parts, beside = ranks(pair.astype(kind), axis, beside)
    parts = [part.astype(F32) for part in parts]
    order, at = range(len(parts)), lax.axis_index(axis)
    if backward:
        order, at = [len(parts) - 1 - j for j in order], len(parts) - 1 - at
    gone = jnp.stack([jnp.zeros_like(pair[0]), jnp.ones_like(pair[1])])
    mine = gone
    for place, j in enumerate(order):
        mine = jnp.where(at == place, gone, mine)
        gone = jnp.stack([parts[j][0] + parts[j][1] * gone[0], parts[j][1] * gone[1]])
    return (gone, mine, *beside)


def carry_planes(pair, inner, backward, beside=()):
    sent = pair.astype(BF16)
    steps = []
    for far in range(1, PLANES):
        if backward:
            route = [(j + far, j) for j in range(PLANES - far)]
        else:
            route = [(j, j + far) for j in range(PLANES - far)]
        steps.append(lax.ppermute(sent if far < PLANES - 1 else sent[:1], "z", route))
    values = tie(*steps, *beside)
    steps, beside = [step.astype(F32) for step in values[: len(steps)]], values[len(steps) :]
    entering = jnp.zeros_like(pair[0])
    for step in reversed(steps):
        entering = step[0] + (step[1] * entering if step.shape[0] == 2 else 0.0)
    for mine in reversed(inner):
        entering = mine[0] + mine[1] * entering
    return (entering, *beside)


def norm(v, gain):
    scale = lax.rsqrt(jnp.mean(v * v, axis=-1, keepdims=True) + 1e-6)
    return v * scale * gain, scale


def norm_back(v, scale, gain, d_out):
    scaled = gain * d_out
    mean = jnp.mean(v * scaled, axis=-1, keepdims=True)
    return scale * scaled - v * (scale * scale * scale * mean), jnp.sum(v * scale * d_out, axis=0)


def body(
    block_input, cotangent, seq_lengths, pre_gain, w_branch, b_branch, w_recur, b_recur, conv_kernel, conv_bias,
    input_gate_weight, input_gate_bias, decay_gate_weight, decay_gate_bias, decay_base, w_output, b_output,
    ffn_gain, w_expand, b_expand, w_shrink, b_shrink,
):
    mid = lax.axis_size("x")
    groups = PLANES * mid * CORES
    place = lax.axis_index(DP)
    side = lax.axis_index("y")
    seqs, pieces, width = block_input.shape
    rows = seqs * pieces
    taps, heads, head_part = conv_kernel.shape
    head_size = head_part * groups
    channels = heads * head_size
    part = w_recur.shape[0]
    units = w_shrink.shape[1]
    halo = (taps - 1) * seqs

    x_low = block_input.transpose(1, 0, 2).reshape(rows, width)
    positions = place * pieces + lax.broadcasted_iota(jnp.int32, (pieces, seqs), 0)
    mask = (positions < seq_lengths[None, :]).reshape(rows, 1)
    d_out = jnp.where(mask, cotangent.transpose(1, 0, 2).reshape(rows, width), 0).astype(BF16)
    early = lax.ppermute(x_low[rows - halo :], DP, [(j, j + 1) for j in range(groups - 1)])

    recur_stack = lax.all_gather(jnp.stack([w_recur, w_branch, w_output]), DP, axis=1, tiled=True)
    inlet_full = lax.all_gather(input_gate_weight.transpose(1, 0, 2).reshape(head_part, channels), DP, axis=0, tiled=True)
    decay_full = lax.all_gather(decay_gate_weight.transpose(1, 0, 2).reshape(head_part, channels), DP, axis=0, tiled=True)
    vectors = jnp.stack([b_branch, b_recur, *[conv_kernel[k] for k in range(taps)], conv_bias, input_gate_bias,
                         decay_gate_bias, decay_base])
    flat = jnp.concatenate([vectors.reshape(-1), pre_gain, b_output, ffn_gain, b_shrink, b_expand.reshape(-1)])
    every = lax.all_gather(flat, DP, axis=0, tiled=False).astype(F32)
    taken = 0

    def take(count):
        nonlocal taken
        taken += count
        return every[:, taken - count : taken]

    by_head = take(vectors.size).reshape(groups, -1, head_part).transpose(1, 0, 2).reshape(-1, channels)
    vec_branch, vec_recur, vec_taps = by_head[0], by_head[1], by_head[2 : 2 + taps]
    vec_base = by_head[5 + taps]
    gain_one, vec_output, gain_two, vec_shrink = [take(part).reshape(width) for _ in range(4)]
    blocks = b_expand.shape[1]
    vec_expand = take(2 * blocks * head_part).reshape(groups, 2, blocks, head_part).transpose(1, 2, 0, 3).reshape(2, units)
    gain_one, gain_two = 1.0 + gain_one, 1.0 + gain_two
    rates = jnp.stack([-8.0 * jax.nn.softplus(vec_base), -8.0 * jax.nn.sigmoid(vec_base)])
    coefs = jnp.concatenate([by_head[2 : 5 + taps], rates], axis=0)
    coefs = jnp.pad(coefs, ((0, 16 - coefs.shape[0]), (0, 0)))

    first = (place == 0).astype(jnp.int32).reshape(1)
    x_ext = jnp.concatenate([early, x_low], axis=0).astype(F32)
    normed_f, _ = norm(x_ext, gain_one)
    normed_ext = normed_f.astype(BF16)
    d_own, d_side = halves(d_out, "y")

    slices = mid * CORES
    tiles = units // LANES
    wide_tiles = -(-tiles // slices)
    wide = wide_tiles * LANES
    starts = [j * (tiles - wide_tiles) // (slices - 1) for j in range(slices)]
    owned = [(starts[j + 1] if j + 1 < slices else tiles) - starts[j] for j in range(slices)]
    chunks = CHUNKS if wide % (CHUNKS * LANES) == 0 else 1
    step = wide // chunks
    sent = []
    for j in range(slices):
        for k in range(chunks):
            at = starts[j] * LANES + k * step
            sent += [w_expand[0, :, at : at + step], w_expand[1, :, at : at + step], w_shrink[:, at : at + step]]
    per = 3 * chunks

    def to_send(low, high):
        mine = [jnp.concatenate(sent[j * per + 3 * k : j * per + 3 * k + 3], axis=1) for j in range(slices) for k in range(low, high)]
        return jnp.stack(mine).reshape(slices, high - low, part, 3 * step)

    def to_plane(mine):
        got = to_slices(mine)
        return [got[:, k].reshape(slices * part, 3 * step) for k in range(got.shape[1])]

    early_chunks = 1
    held = to_plane(to_send(0, early_chunks))
    later = to_send(early_chunks, chunks) if early_chunks < chunks else held[0]
    my_slice = lax.axis_index(("x", "c"))
    my_start = jnp.array(starts, jnp.int32)[my_slice] * LANES
    my_owned = jnp.array(owned, jnp.int32)[my_slice] * LANES
    my_bias = lax.dynamic_slice_in_dim(vec_expand, my_start, wide, 1)
    recur_stack, normed_ext, coefs, inlet_full, decay_full, my_bias, d_out, d_own, d_side, later, *held = tie(
        recur_stack, normed_ext, coefs, inlet_full, decay_full, my_bias, d_out, d_own, d_side, later, *held
    )
    recur_full, branch_full, output_full = recur_stack[0], recur_stack[1], recur_stack[2]
    if early_chunks < chunks:
        held += to_plane(later)
    ffn_full = [lax.all_gather(weights, "z", axis=0, tiled=True) for weights in held]

    d_plane = gather_rows(replicated_plane(d_own, d_side), "c")

    gates, states, branch_back, core_back = head_calls(heads, head_size, rows, rows + halo, seqs, taps)
    normed = normed_ext[halo:]
    recur = dot(normed_ext, recur_full) + vec_recur
    ext_row = lax.broadcasted_iota(jnp.int32, (rows + halo, 1), 0)
    recur = jnp.where(jnp.logical_and(ext_row < halo, place == 0), 0.0, recur)
    conv, sig_in, sig_dec, end, total = gates(first, recur, coefs, inlet_full, decay_full)
    ends, by_core = carry_axis(jnp.stack([end, total]), "c", F32, False)
    ends, by_mid = carry_axis(ends, "x", BF16, False)
    (carry,) = carry_planes(ends, (by_core, by_mid), False)
    branch = dot(normed, branch_full) + vec_branch
    state, mixed = states(first, conv, sig_in, sig_dec, branch, coefs, carry)
    mixed_own, mixed_other = halves(mixed, "y")
    out_other = dot(mixed_other, output_full, ((1,), (1,))).astype(BF16)
    got = swap(out_other, "y")
    out_own = dot(mixed_own, output_full, ((1,), (1,)))
    x_own, _ = halves(x_low, "y")
    x_own = x_own.astype(F32)
    middle = x_own + out_own + got.astype(F32) + vec_output
    second_f, scale_two = norm(middle, gain_two)
    second = second_f.astype(BF16)

    pair = gather_plane(second)
    plane = gather_rows(pair, "c")
    hidden, d_pre, ffn_grads, bias_grads = [], [], [], []
    owned_units = my_owned.reshape(1)
    mixed, normed, plane = tie(mixed, normed, plane)
    normed_dealt, mixed_group = deal_group(normed.T), gather_group(mixed)
    for k in range(chunks):
        bias = my_bias[:, k * step : (k + 1) * step].reshape(1, 2 * step)
        if k == chunks - 1:
            ffn_full[k], normed_dealt, mixed_group, *bias_grads = tie(ffn_full[k], normed_dealt, mixed_group, *bias_grads)
        hid, pre = feed(owned_units, plane, d_plane, ffn_full[k], bias, k * step)
        hidden.append(hid)
        d_pre.append(pre)
        if k + 1 < chunks:
            grads, sums = feed_grads(plane, d_plane, pre, hid)
            ffn_grads.append(grads)
            bias_grads.append(sums)

    def pair_sum(values, block):
        other = feed_back(values, ffn_full, 1, block, CORES)
        own = feed_back(values, ffn_full, 0, block, CORES)
        arrived, own = tie(swap(other, "c"), own)
        return (own.astype(F32) + arrived.astype(F32)).astype(BF16)

    d_pair = pair_sum(d_pre, 0)
    d_pair, *hidden = tie(d_pair, *hidden)
    last_grads, last_sums = feed_grads(plane, d_plane, d_pre[-1], hidden[-1])
    d_second_own, last_sums = scatter_plane(d_pair, last_sums)
    bias_grads = [sums[0].reshape(2, step) for sums in [*bias_grads, last_sums]]
    ffn_grads = [sum_line(grad) for grad in ffn_grads]
    d_middle, grad_gain_two = norm_back(middle, scale_two, gain_two, d_second_own)
    d_middle = d_middle + d_own.astype(F32)
    d_low_own = d_middle.astype(BF16)
    dealt_own = deal_group(d_low_own.T)
    low_other, dealt_own = tie(swap(d_low_own, "y"), dealt_own)
    is_low = side == 0
    d_low = jnp.concatenate([jnp.where(is_low, d_low_own, low_other), jnp.where(is_low, low_other, d_low_own)], axis=0)
    d_mixed = dot(d_low, output_full)
    pulled, d_branch, end_back, branch_sum = branch_back(d_mixed, branch, state, sig_dec, coefs)
    dealt_other = swap(dealt_own, "y")

    def by_plane(grad):
        return grad.astype(BF16).reshape(PLANES, part, channels)

    def by_owner(grad):
        return grad.reshape(groups, -1, channels)

    end_back, last_grads, *ffn_grads = tie(end_back, last_grads, *ffn_grads)
    ffn_grads.append(sum_line(last_grads))
    ends, by_core, *hidden = carry_axis(jnp.stack([end_back, total]), "c", F32, True, hidden)
    out_far, out_near = [feed_back(hidden, ffn_full, j, 2, CORES) for j in (1, 0)]
    ends, by_mid, out_far, d_branch = carry_axis(ends, "x", BF16, True, (out_far, d_branch))
    late, out_near, mixed_group = carry_planes(ends, (by_core, by_mid), True, (out_near, mixed_group))
    out_pair = (out_near.astype(F32) + swap(out_far, "c").astype(F32)).astype(BF16)
    out_side = scatter_side(out_pair) if mid == 2 else (scatter_side(out_pair),)
    d_conv, grad_inlet, grad_decay, core_sums = core_back(
        first, pulled, conv, sig_in, sig_dec, state, recur, coefs, carry, late, inlet_full, decay_full
    )
    branch_group = gather_group(d_branch)
    d_conv, branch_group = tie(d_conv, branch_group)
    behind = lax.ppermute(d_conv[:halo].astype(BF16), DP, [(j + 1, j) for j in range(groups - 1)])
    d_ext = jnp.concatenate([d_conv, behind.astype(F32)], axis=0)
    d_recur = vec_taps[0] * d_ext[:rows]
    for k in range(1, taps):
        d_recur = d_recur + vec_taps[k] * d_ext[k * seqs : k * seqs + rows]
    d_recur = d_recur.astype(BF16)
    recur_near = swap(d_recur, "x") if mid == 2 else lax.all_gather(d_recur, "x", axis=0, tiled=True)
    gates_b = fold_mid(fold_cores(jnp.concatenate([by_owner(grad_inlet), by_owner(grad_decay)], axis=1)))
    recur_near, dealt_other, *out_side = tie(recur_near, dealt_other, *out_side)
    mixed_sides = [lax.dynamic_index_in_dim(mixed_group.reshape(mid * CORES, 2, -1, channels), j, 1, keepdims=False)
                   .reshape(-1, channels) for j in (side, 1 - side)]
    grad_output = dot(dealt_own, mixed_sides[0]) + dot(dealt_other, mixed_sides[1])
    grad_branch = dot(normed_dealt, branch_group)
    packed = [by_plane(grad_output), by_plane(grad_branch)]
    recur_near = jnp.concatenate([d_recur, recur_near], axis=0) if mid == 2 else recur_near
    packed += [by_plane(dot(normed_dealt, gather_rows(recur_near, "c"))), gates_b]
    packed = jnp.concatenate(packed, axis=1)
    packed, d_recur, *ffn_grads = tie(packed, d_recur, *ffn_grads)
    sums = fold_planes(packed)
    d_normed = dot(d_branch, branch_full, ((1,), (1,))) + dot(d_recur, recur_full, ((1,), (1,)))
    dn_own, dn_other = halves(d_normed, "y")
    dn_got = swap(dn_other.astype(BF16), "y")
    dn_own = dn_own + dn_got.astype(F32)
    if mid == 2:
        out_side = [(out_side[0].astype(F32) + out_side[1].astype(F32)).astype(BF16)]
    out_side = out_side[0]
    scale_one = lax.rsqrt(jnp.mean(x_own * x_own, axis=-1, keepdims=True) + 1e-6)
    d_input, grad_gain_one = norm_back(x_own, scale_one, gain_one, dn_own)
    d_input = whole_rows((d_middle + d_input).astype(BF16), "y")

    shared = jnp.stack([grad_gain_one, jnp.sum(d_low_own.astype(F32), axis=0), grad_gain_two])
    shared = shared + swap(shared, "y")
    recur_sum = jnp.sum(d_recur.astype(F32), axis=0)
    by_unit = lax.dynamic_update_slice_in_dim(jnp.zeros((2, units), F32), jnp.concatenate(bias_grads, axis=1), my_start, 1)
    small = jnp.concatenate(
        [
            jnp.concatenate([branch_sum[:1], recur_sum[None], core_sums[4:], core_sums[3:4], core_sums[:3]], axis=0),
            shared.reshape(-1, channels),
            jnp.sum(d_out.astype(F32), axis=0).reshape(-1, channels),
            by_unit.reshape(-1, channels),
        ],
        axis=0,
    )
    small = sum_plane(small)
    returned = jnp.stack([grad.reshape(slices, part, 3 * step) for grad in ffn_grads], axis=1)
    small, returned = tie(small, returned)

    mask_own, _ = halves(mask, "y")
    result = jnp.where(mask_own, middle + scatter_rows(out_side, "x").astype(F32) + vec_shrink, 0.0).astype(BF16)
    result = whole_rows(result, "y")
    small = sum_planes(small)
    count = 6 + taps
    head_sums = lax.dynamic_slice_in_dim(small[:count].reshape(count, heads, head_size), place * head_part, head_part, 2)
    features = 4 * (width // channels)
    feature_sums = lax.dynamic_slice_in_dim(small[count : count + features].reshape(4, width), place * part, part, 1)
    unit_sums = small[count + features :].reshape(2, blocks, head_size)
    g_b_expand = lax.dynamic_slice_in_dim(unit_sums, place * head_part, head_part, 2)
    g_b_branch, g_b_recur, g_kernel = head_sums[0], head_sums[1], head_sums[2 : 2 + taps]
    g_conv_bias, g_b_inlet, g_b_decay, g_base = [head_sums[2 + taps + j] for j in range(4)]
    g_pre_gain, g_b_output, g_ffn_gain, g_b_shrink = [feature_sums[j] for j in range(4)]

    ffn_sum = to_slices(returned)
    grads_out = []
    for kind in range(3):
        pieces_out = []
        for j in range(slices):
            for k in range(chunks):
                keep = min(step, owned[j] * LANES - k * step)
                if keep > 0:
                    pieces_out.append(ffn_sum[j, k, :, kind * step : kind * step + keep])
        grads_out.append(jnp.concatenate(pieces_out, axis=1).astype(F32))
    grad_expand = jnp.stack(grads_out[:2])
    grad_shrink = grads_out[2]

    def gate_out(at):
        return sums[at : at + head_part].reshape(head_part, heads, head_size).transpose(1, 0, 2)

    def rows_out(v):
        return v.reshape(pieces, seqs, width).transpose(1, 0, 2)

    return (
        rows_out(result), rows_out(d_input), g_pre_gain, sums[part : 2 * part], g_b_branch, sums[2 * part : 3 * part], g_b_recur,
        g_kernel, g_conv_bias, gate_out(3 * part), g_b_inlet, gate_out(3 * part + head_part), g_b_decay, g_base,
        sums[:part], g_b_output, g_ffn_gain, grad_expand, g_b_expand, grad_shrink, g_b_shrink,
    )


def solution(mesh):
    groups, sides = mesh.shape["dp"], mesh.shape["tensor"]
    mid = groups // (PLANES * CORES)
    grid = Mesh(mesh.devices.reshape(PLANES, mid, CORES, sides), ("z", "x", "c", "y"))
    rows, vec = P(None, DP, None), P(DP)
    mat, head, tap, gate = P(DP, "y"), P("y", DP), P(None, "y", DP), P("y", DP, None)
    wide = P(None, DP, "y")
    return jax.shard_map(
        body,
        mesh=grid,
        in_specs=(
            rows, rows, P(), vec, mat, head, mat, head, tap, head, gate, head, gate, head, head, mat, vec, vec,
            wide, tap, mat, vec,
        ),
        out_specs=(
            rows, rows, vec, mat, head, mat, head, tap, head, gate, head, gate, head, head, mat, vec, vec,
            wide, tap, mat, vec,
        ),
        check_vma=False,
    )
```

```python
import functools

import jax
import jax.numpy as jnp
from jax import lax
from jax.experimental import pallas as pl
from jax.experimental.pallas import tpu as pltpu
from jax.sharding import Mesh, PartitionSpec as P

F32, BF16 = jnp.float32, jnp.bfloat16
LANES = 128
PLANES = 4
CORES = 2
CHUNKS = 2
VMEM_BYTES = 56 * 1024 * 1024
SMALL = pl.CostEstimate(flops=1, bytes_accessed=1, transcendentals=0)
DP = ("z", "x", "c")
GELU_A, GELU_B = 0.7978845608028654, 0.044715


def gelu_parts(v):
    square = v * v
    bent = jnp.tanh(GELU_A * v * (1.0 + GELU_B * square))
    half = 0.5 * (1.0 + bent)
    slope = half + 0.5 * v * (1.0 - bent * bent) * (GELU_A * (1.0 + 3.0 * GELU_B * square))
    return v * half, slope


def gelu(v):
    return v * (0.5 * (1.0 + jnp.tanh(GELU_A * v * (1.0 + GELU_B * v * v))))


def dot(a, b, dims=((1,), (0,))):
    return lax.dot_general(a, b, (dims, ((), ())), preferred_element_type=F32)


def tie(*values):
    return lax.optimization_barrier(values)


def input_scale(decay, at_start):
    spare = 1.0 - decay * decay
    scale = jnp.sqrt(jnp.maximum(spare, 0.001))
    return jnp.where(at_start, 1.0, scale), spare


def start_rows(first_ref, rows, seqs, width):
    row = lax.broadcasted_iota(jnp.int32, (rows, width), 0)
    return jnp.logical_and(row < seqs, first_ref[0] == 1)


def gates_kernel(first_ref, r_ref, v_ref, wi_ref, wd_ref, c_ref, si_ref, sd_ref, e_ref, p_ref, *, seqs, taps):
    rows, width = c_ref.shape
    halo = r_ref.shape[0] - rows
    conv = v_ref[taps : taps + 1, :] + v_ref[0:1, :] * r_ref[pl.ds(halo, rows), :]
    for k in range(1, taps):
        conv = conv + v_ref[k : k + 1, :] * r_ref[pl.ds(halo - k * seqs, rows), :]
    c_ref[...] = conv
    low = conv.astype(BF16)
    si = jax.nn.sigmoid(dot(low, wi_ref[...]) + v_ref[taps + 1 : taps + 2, :])
    sd = jax.nn.sigmoid(dot(low, wd_ref[...]) + v_ref[taps + 2 : taps + 3, :])
    si_ref[...] = si
    sd_ref[...] = sd
    decay = jnp.exp(sd * v_ref[taps + 3 : taps + 4, :])
    scale, _ = input_scale(decay, start_rows(first_ref, rows, seqs, width))
    source = conv * si * scale
    state, total = source[:seqs], decay[:seqs]
    for p in range(1, rows // seqs):
        a = decay[p * seqs : (p + 1) * seqs]
        state = a * state + source[p * seqs : (p + 1) * seqs]
        total = total * a
    e_ref[...] = state
    p_ref[...] = total


def states_kernel(first_ref, c_ref, si_ref, sd_ref, b_ref, v_ref, carry_ref, s_ref, m_ref, *, seqs, taps):
    rows, width = c_ref.shape
    decay = jnp.exp(sd_ref[...] * v_ref[taps + 3 : taps + 4, :])
    scale, _ = input_scale(decay, start_rows(first_ref, rows, seqs, width))
    source = c_ref[...] * si_ref[...] * scale
    state = carry_ref[...]
    for p in range(rows // seqs):
        at = slice(p * seqs, (p + 1) * seqs)
        state = decay[at] * state + source[at]
        s_ref[pl.ds(p * seqs, seqs), :] = state
    m_ref[...] = (gelu(b_ref[...]) * s_ref[...]).astype(BF16)


def branch_kernel(dm_ref, b_ref, s_ref, sd_ref, v_ref, t_ref, db_ref, e_ref, sum_ref, *, seqs, taps):
    rows, _ = t_ref.shape
    value, slope = gelu_parts(b_ref[...])
    dm = dm_ref[...]
    t = dm * value
    t_ref[...] = t
    db = (dm * s_ref[...] * slope).astype(BF16)
    db_ref[...] = db
    sum_ref[...] = jnp.broadcast_to(jnp.sum(db.astype(F32), axis=0, keepdims=True), sum_ref.shape)
    decay = jnp.exp(sd_ref[...] * v_ref[taps + 3 : taps + 4, :])
    count = rows // seqs
    grad = t[(count - 1) * seqs :]
    for p in range(count - 2, -1, -1):
        grad = t[p * seqs : (p + 1) * seqs] + decay[(p + 1) * seqs : (p + 2) * seqs] * grad
    e_ref[...] = decay[:seqs] * grad


def core_kernel(
    first_ref, t_ref, c_ref, si_ref, sd_ref, s_ref, r_ref, v_ref, carry_ref, late_ref, wi_ref, wd_ref,
    dc_ref, gi_ref, gd_ref, sum_ref, ds_ref, *, seqs, taps,
):
    rows, width = c_ref.shape
    halo = r_ref.shape[0] - rows
    count = rows // seqs
    si, sd, conv = si_ref[...], sd_ref[...], c_ref[...]
    rate = v_ref[taps + 3 : taps + 4, :]
    decay = jnp.exp(sd * rate)
    at_start = start_rows(first_ref, rows, seqs, width)
    scale, spare = input_scale(decay, at_start)
    grad = late_ref[...]
    for p in range(count - 1, -1, -1):
        grad = t_ref[pl.ds(p * seqs, seqs), :] + grad
        ds_ref[pl.ds(p * seqs, seqs), :] = grad
        grad = decay[p * seqs : (p + 1) * seqs] * grad
    ds = ds_ref[...]
    before = carry_ref[...] if count == 1 else jnp.concatenate([carry_ref[...], s_ref[pl.ds(0, rows - seqs), :]], axis=0)
    bends = jnp.logical_and(spare > 0.001, jnp.logical_not(at_start))
    d_scale = jnp.where(bends, -(decay * decay) / scale, 0.0)
    gated = ds * conv
    d_log = ds * before * decay + gated * si * d_scale
    d_in = (gated * scale * si * (1.0 - si)).astype(BF16)
    d_dec = (d_log * rate * sd * (1.0 - sd)).astype(BF16)
    low = conv.astype(BF16)
    gi_ref[...] = dot(low, d_in, ((0,), (0,))).astype(gi_ref.dtype)
    gd_ref[...] = dot(low, d_dec, ((0,), (0,))).astype(gd_ref.dtype)
    dc = ds * si * scale + dot(d_in, wi_ref[...], ((1,), (1,))) + dot(d_dec, wd_ref[...], ((1,), (1,)))
    dc_ref[...] = dc

    def total(values):
        return jnp.sum(values, axis=0, keepdims=True)

    parts = [
        total(d_in.astype(F32)),
        total(d_dec.astype(F32)),
        total(d_log * sd) * v_ref[taps + 4 : taps + 5, :],
        total(dc),
    ]
    for k in range(taps):
        parts.append(total(r_ref[pl.ds(halo - k * seqs, rows), :] * dc))
    sum_ref[...] = jnp.concatenate(parts, axis=0)


def head_calls(heads, width, rows, halo_rows, seqs, taps):
    def cols(n):
        return pl.BlockSpec((n, width), lambda h: (0, h))

    flag = pl.BlockSpec(memory_space=pltpu.SMEM)
    full = heads * width
    params = pltpu.CompilerParams(vmem_limit_bytes=48 * 1024 * 1024)
    vec_rows = 16

    def shape(n, kind=F32):
        return jax.ShapeDtypeStruct((n, full), kind)

    def call(kernel, ins, outs, shapes, scratch=(), flops=0):
        return pl.pallas_call(
            functools.partial(kernel, seqs=seqs, taps=taps),
            grid=(heads,),
            in_specs=ins,
            out_specs=outs,
            out_shape=shapes,
            scratch_shapes=list(scratch),
            compiler_params=params,
            cost_estimate=SMALL,
        )

    unit = 2 * rows * full * width
    return (
        call(
            gates_kernel,
            [flag, cols(halo_rows), cols(vec_rows), cols(width), cols(width)],
            [cols(rows), cols(rows), cols(rows), cols(seqs), cols(seqs)],
            [shape(rows), shape(rows), shape(rows), shape(seqs), shape(seqs)],
            flops=2 * unit,
        ),
        call(
            states_kernel,
            [flag, cols(rows), cols(rows), cols(rows), cols(rows), cols(vec_rows), cols(seqs)],
            [cols(rows), cols(rows)],
            [shape(rows), shape(rows, BF16)],
        ),
        call(
            branch_kernel,
            [cols(rows), cols(rows), cols(rows), cols(rows), cols(vec_rows)],
            [cols(rows), cols(rows), cols(seqs), cols(8)],
            [shape(rows), shape(rows, BF16), shape(seqs), shape(8)],
        ),
        call(
            core_kernel,
            [flag, cols(rows), cols(rows), cols(rows), cols(rows), cols(rows), cols(halo_rows), cols(vec_rows),
             cols(seqs), cols(seqs), cols(width), cols(width)],
            [cols(rows), cols(width), cols(width), cols(4 + taps)],
            [shape(rows), shape(width, BF16), shape(width, BF16), shape(4 + taps)],
            scratch=[pltpu.VMEM((rows, width), F32)],
            flops=4 * unit,
        ),
    )


def row_tile(rows):
    return max(n for n in (512, 256, 128, 64, 32, 16) if rows % n == 0)


def feed_kernel(at_ref, x_ref, d_ref, w_ref, b_ref, h_ref, g_ref, *, first_unit):
    step = h_ref.shape[1]
    pre = dot(x_ref[...], w_ref[:, : 2 * step]) + b_ref[...]
    d_hidden = dot(d_ref[...], w_ref[:, 2 * step :])
    gate, up = pre[:, :step], pre[:, step:]
    mine = lax.broadcasted_iota(jnp.int32, gate.shape, 1) + first_unit < at_ref[0]
    value, slope = gelu_parts(gate)
    h_ref[...] = jnp.where(mine, value * up, 0.0).astype(BF16)
    g_ref[:, :step] = jnp.where(mine, d_hidden * up * slope, 0.0).astype(BF16)
    g_ref[:, step:] = jnp.where(mine, d_hidden * value, 0.0).astype(BF16)


def feed(owned, x, d, weights, bias, first_unit):
    rows, width = x.shape
    step = weights.shape[1] // 3
    tile = row_tile(rows)
    return pl.pallas_call(
        functools.partial(feed_kernel, first_unit=first_unit),
        grid=(rows // tile,),
        in_specs=[
            pl.BlockSpec(memory_space=pltpu.SMEM),
            pl.BlockSpec((tile, width), lambda i: (i, 0)),
            pl.BlockSpec((tile, width), lambda i: (i, 0)),
            pl.BlockSpec((width, 3 * step), lambda i: (0, 0)),
            pl.BlockSpec((1, 2 * step), lambda i: (0, 0)),
        ],
        out_specs=[
            pl.BlockSpec((tile, step), lambda i: (i, 0)),
            pl.BlockSpec((tile, 2 * step), lambda i: (i, 0)),
        ],
        out_shape=[
            jax.ShapeDtypeStruct((rows, step), BF16),
            jax.ShapeDtypeStruct((rows, 2 * step), BF16),
        ],
        compiler_params=pltpu.CompilerParams(vmem_limit_bytes=VMEM_BYTES),
        cost_estimate=SMALL,
    )(owned, x, d, weights, bias)


def grad_kernel(x_ref, d_ref, g_ref, h_ref, o_ref, sum_ref):
    step = h_ref.shape[1]

    @pl.when(pl.program_id(0) == 0)
    def _():
        total = jnp.sum(g_ref[...].astype(F32), axis=0, keepdims=True)
        sum_ref[...] = jnp.broadcast_to(total, sum_ref.shape)

    o_ref[:, : 2 * step] = dot(x_ref[...], g_ref[...], ((0,), (0,))).astype(BF16)
    o_ref[:, 2 * step :] = dot(d_ref[...], h_ref[...], ((0,), (0,))).astype(BF16)


def feed_grads(x, d, d_pre, hidden):
    rows, width = x.shape
    step = hidden.shape[1]
    tile = 512 if width % 512 == 0 else width
    return pl.pallas_call(
        grad_kernel,
        grid=(width // tile,),
        in_specs=[
            pl.BlockSpec((rows, tile), lambda i: (0, i)),
            pl.BlockSpec((rows, tile), lambda i: (0, i)),
            pl.BlockSpec((rows, 2 * step), lambda i: (0, 0)),
            pl.BlockSpec((rows, step), lambda i: (0, 0)),
        ],
        out_specs=[pl.BlockSpec((tile, 3 * step), lambda i: (i, 0)), pl.BlockSpec((8, 2 * step), lambda i: (0, 0))],
        out_shape=[jax.ShapeDtypeStruct((width, 3 * step), BF16), jax.ShapeDtypeStruct((8, 2 * step), F32)],
        compiler_params=pltpu.CompilerParams(vmem_limit_bytes=VMEM_BYTES),
        cost_estimate=SMALL,
    )(x, d, d_pre, hidden)


def back_kernel(*refs):
    count = (len(refs) - 1) // 2
    out = dot(refs[0][...], refs[count][...], ((1,), (1,)))
    for k in range(1, count):
        out = out + dot(refs[k][...], refs[count + k][...], ((1,), (1,)))
    refs[-1][...] = out.astype(BF16)


def feed_back(values, weights, part, block, blocks):
    rows, cols = values[0].shape
    rows = rows // blocks
    width = weights[0].shape[0]
    tile = 512 if width % 512 == 0 else width
    return pl.pallas_call(
        back_kernel,
        grid=(width // tile,),
        in_specs=[pl.BlockSpec((rows, cols), lambda i: (part, 0)) for _ in values]
        + [pl.BlockSpec((tile, cols), lambda i: (i, block)) for _ in weights],
        out_specs=pl.BlockSpec((rows, tile), lambda i: (0, i)),
        out_shape=jax.ShapeDtypeStruct((rows, width), BF16),
        compiler_params=pltpu.CompilerParams(vmem_limit_bytes=VMEM_BYTES),
        cost_estimate=SMALL,
    )(*values, *weights)


def swap(v, axis):
    return lax.ppermute(v, axis, [(0, 1), (1, 0)])


def gather_rows(v, axis):
    if lax.axis_size(axis) == 2:
        return jnp.concatenate([v, swap(v, axis)], axis=0)
    return lax.all_gather(v, axis, axis=0, tiled=True)


def scatter_rows(v, axis):
    if lax.axis_size(axis) == 2:
        half = v.shape[0] // 2
        return (v[:half].astype(F32) + swap(v[half:], axis).astype(F32)).astype(BF16)
    return lax.psum_scatter(v, axis, scatter_dimension=0, tiled=True)


def gather_plane(v):
    if lax.axis_size("x") != 2:
        return gather_rows(gather_rows(v, "x"), "y")
    half = v.shape[0] // 2
    a, b = v[:half], v[half:]
    ax, by = swap(a, "x"), swap(b, "y")
    a, b = jnp.concatenate([a, ax], axis=0), jnp.concatenate([b, by], axis=0)
    return jnp.concatenate([a, swap(a, "y"), b, swap(b, "x")], axis=0)


def replicated_plane(own, side):
    if lax.axis_size("x") != 2:
        return gather_plane(own)
    half = own.shape[0] // 2
    near = swap(own, "x")
    far = swap(near, "y")
    return jnp.concatenate(
        [own[:half], near[:half], side[:half], far[:half], own[half:], side[half:], near[half:], far[half:]], axis=0
    )


def scatter_plane(v, *beside):
    if lax.axis_size("x") != 2:
        return (scatter_rows(scatter_rows(v, "y"), "x").astype(F32), *beside)
    half = v.shape[0] // 2
    quarter = half // 2
    a = v[:half].reshape(2, 2, quarter // 2, -1).swapaxes(0, 1).reshape(half, -1)
    b = v[half:].reshape(2, 2, quarter // 2, -1).swapaxes(0, 1).reshape(half, -1)
    got_a, got_b, *beside = tie(swap(a[quarter:], "x"), swap(b[quarter:], "y"), *beside)

    def fold(rows, got):
        return rows.astype(F32) + got.astype(F32)

    a, b = fold(a[:quarter], got_a).astype(BF16), fold(b[:quarter], got_b).astype(BF16)
    keep = quarter // 2
    a, b = fold(a[:keep], swap(a[keep:], "y")), fold(b[:keep], swap(b[keep:], "x"))
    return (jnp.concatenate([a, b], axis=0), *beside)


def scatter_side(v):
    if lax.axis_size("x") != 2:
        return scatter_rows(v, "y")
    count = v.shape[0] // 8
    a, b = v[: 4 * count].reshape(4, count, -1), v[4 * count :].reshape(4, count, -1)
    keep = jnp.concatenate([a[0], b[0], a[1], b[2]], axis=0)
    send = jnp.concatenate([a[2], b[1], a[3], b[3]], axis=0)
    return keep, swap(send, "y")


def gather_group(v):
    return gather_rows(gather_rows(v, "x"), "c")


def deal_group(v):
    mid, count = lax.axis_size("x"), v.shape[1]
    v = v.reshape(PLANES, mid * CORES, -1, count)
    if mid != 2:
        got = lax.all_gather(v, "x", axis=3, tiled=True)
        got = gather_cols(got)
        return lax.dynamic_index_in_dim(got, lax.axis_index(("x", "c")), 1, keepdims=False).reshape(-1, got.shape[-1])
    me = lax.axis_index(("x", "c"))
    parts = []
    for flip in (0, 2, 1, 3):
        part = lax.dynamic_index_in_dim(v, jnp.bitwise_xor(me, flip), 1, keepdims=False)
        parts.append(lax.ppermute(part, ("x", "c"), [(j, j ^ flip) for j in range(4)]) if flip else part)
    return jnp.concatenate(parts, axis=-1).reshape(-1, 4 * count)


def gather_cols(v):
    return jnp.concatenate([v, swap(v, "c")], axis=-1)


def fold_cores(v):
    v = v.reshape(lax.axis_size("z"), lax.axis_size("x"), CORES, *v.shape[1:])
    at = lax.axis_index("c")
    own = lax.dynamic_index_in_dim(v, at, 2, keepdims=False)
    return (own.astype(F32) + swap(lax.dynamic_index_in_dim(v, 1 - at, 2, keepdims=False), "c").astype(F32)).astype(BF16)


def fold_mid(v):
    if lax.axis_size("x") != 2:
        return lax.psum_scatter(v, "x", scatter_dimension=1, tiled=False)
    at = lax.axis_index("x")
    own = lax.dynamic_index_in_dim(v, at, 1, keepdims=False)
    return (own.astype(F32) + swap(lax.dynamic_index_in_dim(v, 1 - at, 1, keepdims=False), "x").astype(F32)).astype(BF16)


def fold_planes(v):
    return lax.psum_scatter(v, "z", scatter_dimension=0, tiled=False).astype(F32)


def sum_plane(v):
    if lax.axis_size("x") != 2:
        v = v + swap(v, "c")
        return lax.psum(v, "x")
    return sum([lax.ppermute(v, ("x", "c"), [(j, j ^ flip) for j in range(4)]) for flip in (1, 2, 3)], v)


def sum_planes(v):
    count = lax.axis_size("z")
    return sum([lax.ppermute(v, "z", [(j, (j + far) % count) for j in range(count)]) for far in range(1, count)], v)


def sum_line(v):
    return lax.psum_scatter(v, "z", scatter_dimension=0, tiled=True)


def to_slices(v):
    if lax.axis_size("x") != 2:
        return lax.all_to_all(v, ("x", "c"), split_axis=0, concat_axis=0, tiled=True)
    me = lax.axis_index(("x", "c"))
    pick = functools.partial(lax.dynamic_slice_in_dim, slice_size=1, axis=0)
    out = lax.dynamic_update_slice_in_dim(jnp.zeros_like(v), pick(v, me), me, 0)
    for flip in (1, 2, 3):
        other = jnp.bitwise_xor(me, flip)
        got = lax.ppermute(pick(v, other), ("x", "c"), [(j, j ^ flip) for j in range(4)])
        out = lax.dynamic_update_slice_in_dim(out, got, other, 0)
    return out


def halves(v, axis):
    half = v.shape[0] // 2
    at = lax.axis_index(axis)
    own = lax.dynamic_slice_in_dim(v, at * half, half, 0)
    return own, lax.dynamic_slice_in_dim(v, (1 - at) * half, half, 0)


def whole_rows(own, axis):
    other = swap(own, axis)
    low = lax.axis_index(axis) == 0
    return jnp.concatenate([jnp.where(low, own, other), jnp.where(low, other, own)], axis=0)


def ranks(value, axis, beside):
    count = lax.axis_size(axis)
    if count == 2:
        other, *beside = tie(swap(value, axis), *beside)
        low = lax.axis_index(axis) == 0
        return [jnp.where(low, value, other), jnp.where(low, other, value)], beside
    every, *beside = tie(lax.all_gather(value, axis), *beside)
    return [every[j] for j in range(count)], beside


def carry_axis(pair, axis, kind, backward, beside=()):
    parts, beside = ranks(pair.astype(kind), axis, beside)
    parts = [part.astype(F32) for part in parts]
    order, at = range(len(parts)), lax.axis_index(axis)
    if backward:
        order, at = [len(parts) - 1 - j for j in order], len(parts) - 1 - at
    gone = jnp.stack([jnp.zeros_like(pair[0]), jnp.ones_like(pair[1])])
    mine = gone
    for place, j in enumerate(order):
        mine = jnp.where(at == place, gone, mine)
        gone = jnp.stack([parts[j][0] + parts[j][1] * gone[0], parts[j][1] * gone[1]])
    return (gone, mine, *beside)


def carry_planes(pair, inner, backward, beside=()):
    sent = pair.astype(BF16)
    steps = []
    for far in range(1, PLANES):
        if backward:
            route = [(j + far, j) for j in range(PLANES - far)]
        else:
            route = [(j, j + far) for j in range(PLANES - far)]
        steps.append(lax.ppermute(sent if far < PLANES - 1 else sent[:1], "z", route))
    values = tie(*steps, *beside)
    steps, beside = [step.astype(F32) for step in values[: len(steps)]], values[len(steps) :]
    entering = jnp.zeros_like(pair[0])
    for step in reversed(steps):
        entering = step[0] + (step[1] * entering if step.shape[0] == 2 else 0.0)
    for mine in reversed(inner):
        entering = mine[0] + mine[1] * entering
    return (entering, *beside)


def norm(v, gain):
    scale = lax.rsqrt(jnp.mean(v * v, axis=-1, keepdims=True) + 1e-6)
    return v * scale * gain, scale


def norm_back(v, scale, gain, d_out):
    scaled = gain * d_out
    mean = jnp.mean(v * scaled, axis=-1, keepdims=True)
    return scale * scaled - v * (scale * scale * scale * mean), jnp.sum(v * scale * d_out, axis=0)


def body(
    block_input, cotangent, seq_lengths, pre_gain, w_branch, b_branch, w_recur, b_recur, conv_kernel, conv_bias,
    input_gate_weight, input_gate_bias, decay_gate_weight, decay_gate_bias, decay_base, w_output, b_output,
    ffn_gain, w_expand, b_expand, w_shrink, b_shrink,
):
    mid = lax.axis_size("x")
    groups = PLANES * mid * CORES
    place = lax.axis_index(DP)
    side = lax.axis_index("y")
    seqs, pieces, width = block_input.shape
    rows = seqs * pieces
    taps, heads, head_part = conv_kernel.shape
    head_size = head_part * groups
    channels = heads * head_size
    part = w_recur.shape[0]
    units = w_shrink.shape[1]
    halo = (taps - 1) * seqs

    x_low = block_input.transpose(1, 0, 2).reshape(rows, width)
    positions = place * pieces + lax.broadcasted_iota(jnp.int32, (pieces, seqs), 0)
    mask = (positions < seq_lengths[None, :]).reshape(rows, 1)
    d_out = jnp.where(mask, cotangent.transpose(1, 0, 2).reshape(rows, width), 0).astype(BF16)
    early = lax.ppermute(x_low[rows - halo :], DP, [(j, j + 1) for j in range(groups - 1)])

    recur_stack = lax.all_gather(jnp.stack([w_recur, w_branch, w_output]), DP, axis=1, tiled=True)
    inlet_full = lax.all_gather(input_gate_weight.transpose(1, 0, 2).reshape(head_part, channels), DP, axis=0, tiled=True)
    decay_full = lax.all_gather(decay_gate_weight.transpose(1, 0, 2).reshape(head_part, channels), DP, axis=0, tiled=True)
    vectors = jnp.stack([b_branch, b_recur, *[conv_kernel[k] for k in range(taps)], conv_bias, input_gate_bias,
                         decay_gate_bias, decay_base])
    flat = jnp.concatenate([vectors.reshape(-1), pre_gain, b_output, ffn_gain, b_shrink, b_expand.reshape(-1)])
    every = lax.all_gather(flat, DP, axis=0, tiled=False).astype(F32)
    taken = 0

    def take(count):
        nonlocal taken
        taken += count
        return every[:, taken - count : taken]

    by_head = take(vectors.size).reshape(groups, -1, head_part).transpose(1, 0, 2).reshape(-1, channels)
    vec_branch, vec_recur, vec_taps = by_head[0], by_head[1], by_head[2 : 2 + taps]
    vec_base = by_head[5 + taps]
    gain_one, vec_output, gain_two, vec_shrink = [take(part).reshape(width) for _ in range(4)]
    blocks = b_expand.shape[1]
    vec_expand = take(2 * blocks * head_part).reshape(groups, 2, blocks, head_part).transpose(1, 2, 0, 3).reshape(2, units)
    gain_one, gain_two = 1.0 + gain_one, 1.0 + gain_two
    rates = jnp.stack([-8.0 * jax.nn.softplus(vec_base), -8.0 * jax.nn.sigmoid(vec_base)])
    coefs = jnp.concatenate([by_head[2 : 5 + taps], rates], axis=0)
    coefs = jnp.pad(coefs, ((0, 16 - coefs.shape[0]), (0, 0)))

    first = (place == 0).astype(jnp.int32).reshape(1)
    x_ext = jnp.concatenate([early, x_low], axis=0).astype(F32)
    normed_f, _ = norm(x_ext, gain_one)
    normed_ext = normed_f.astype(BF16)
    d_own, d_side = halves(d_out, "y")

    slices = mid * CORES
    tiles = units // LANES
    wide_tiles = -(-tiles // slices)
    wide = wide_tiles * LANES
    starts = [j * (tiles - wide_tiles) // (slices - 1) for j in range(slices)]
    owned = [(starts[j + 1] if j + 1 < slices else tiles) - starts[j] for j in range(slices)]
    chunks = CHUNKS if wide % (CHUNKS * LANES) == 0 else 1
    step = wide // chunks
    sent = []
    for j in range(slices):
        for k in range(chunks):
            at = starts[j] * LANES + k * step
            sent += [w_expand[0, :, at : at + step], w_expand[1, :, at : at + step], w_shrink[:, at : at + step]]
    per = 3 * chunks

    def to_send(low, high):
        mine = [jnp.concatenate(sent[j * per + 3 * k : j * per + 3 * k + 3], axis=1) for j in range(slices) for k in range(low, high)]
        return jnp.stack(mine).reshape(slices, high - low, part, 3 * step)

    def to_plane(mine):
        got = to_slices(mine)
        return [got[:, k].reshape(slices * part, 3 * step) for k in range(got.shape[1])]

    early_chunks = 1
    held = to_plane(to_send(0, early_chunks))
    later = to_send(early_chunks, chunks) if early_chunks < chunks else held[0]
    my_slice = lax.axis_index(("x", "c"))
    my_start = jnp.array(starts, jnp.int32)[my_slice] * LANES
    my_owned = jnp.array(owned, jnp.int32)[my_slice] * LANES
    my_bias = lax.dynamic_slice_in_dim(vec_expand, my_start, wide, 1)
    recur_stack, normed_ext, coefs, inlet_full, decay_full, my_bias, d_out, d_own, d_side, later, *held = tie(
        recur_stack, normed_ext, coefs, inlet_full, decay_full, my_bias, d_out, d_own, d_side, later, *held
    )
    recur_full, branch_full, output_full = recur_stack[0], recur_stack[1], recur_stack[2]
    if early_chunks < chunks:
        held += to_plane(later)
    ffn_full = [lax.all_gather(weights, "z", axis=0, tiled=True) for weights in held]

    d_plane = gather_rows(replicated_plane(d_own, d_side), "c")

    gates, states, branch_back, core_back = head_calls(heads, head_size, rows, rows + halo, seqs, taps)
    normed = normed_ext[halo:]
    recur = dot(normed_ext, recur_full) + vec_recur
    ext_row = lax.broadcasted_iota(jnp.int32, (rows + halo, 1), 0)
    recur = jnp.where(jnp.logical_and(ext_row < halo, place == 0), 0.0, recur)
    conv, sig_in, sig_dec, end, total = gates(first, recur, coefs, inlet_full, decay_full)
    ends, by_core = carry_axis(jnp.stack([end, total]), "c", F32, False)
    ends, by_mid = carry_axis(ends, "x", BF16, False)
    (carry,) = carry_planes(ends, (by_core, by_mid), False)
    branch = dot(normed, branch_full) + vec_branch
    state, mixed = states(first, conv, sig_in, sig_dec, branch, coefs, carry)
    mixed_own, mixed_other = halves(mixed, "y")
    out_other = dot(mixed_other, output_full, ((1,), (1,))).astype(BF16)
    got = swap(out_other, "y")
    out_own = dot(mixed_own, output_full, ((1,), (1,)))
    x_own, _ = halves(x_low, "y")
    x_own = x_own.astype(F32)
    middle = x_own + out_own + got.astype(F32) + vec_output
    second_f, scale_two = norm(middle, gain_two)
    second = second_f.astype(BF16)

    pair = gather_plane(second)
    plane = gather_rows(pair, "c")
    hidden, d_pre, ffn_grads, bias_grads = [], [], [], []
    owned_units = my_owned.reshape(1)
    mixed, normed, plane = tie(mixed, normed, plane)
    normed_dealt, mixed_group = deal_group(normed.T), gather_group(mixed)
    for k in range(chunks):
        bias = my_bias[:, k * step : (k + 1) * step].reshape(1, 2 * step)
        if k == chunks - 1:
            ffn_full[k], normed_dealt, mixed_group, *bias_grads = tie(ffn_full[k], normed_dealt, mixed_group, *bias_grads)
        hid, pre = feed(owned_units, plane, d_plane, ffn_full[k], bias, k * step)
        hidden.append(hid)
        d_pre.append(pre)
        if k + 1 < chunks:
            grads, sums = feed_grads(plane, d_plane, pre, hid)
            ffn_grads.append(grads)
            bias_grads.append(sums)

    def pair_sum(values, block):
        other = feed_back(values, ffn_full, 1, block, CORES)
        own = feed_back(values, ffn_full, 0, block, CORES)
        arrived, own = tie(swap(other, "c"), own)
        return (own.astype(F32) + arrived.astype(F32)).astype(BF16)

    d_pair = pair_sum(d_pre, 0)
    d_pair, *hidden = tie(d_pair, *hidden)
    last_grads, last_sums = feed_grads(plane, d_plane, d_pre[-1], hidden[-1])
    d_second_own, last_sums = scatter_plane(d_pair, last_sums)
    bias_grads = [sums[0].reshape(2, step) for sums in [*bias_grads, last_sums]]
    ffn_grads = [sum_line(grad) for grad in ffn_grads]
    d_middle, grad_gain_two = norm_back(middle, scale_two, gain_two, d_second_own)
    d_middle = d_middle + d_own.astype(F32)
    d_low_own = d_middle.astype(BF16)
    dealt_own = deal_group(d_low_own.T)
    low_other, dealt_own = tie(swap(d_low_own, "y"), dealt_own)
    is_low = side == 0
    d_low = jnp.concatenate([jnp.where(is_low, d_low_own, low_other), jnp.where(is_low, low_other, d_low_own)], axis=0)
    d_mixed = dot(d_low, output_full)
    pulled, d_branch, end_back, branch_sum = branch_back(d_mixed, branch, state, sig_dec, coefs)
    dealt_other = swap(dealt_own, "y")

    def by_plane(grad):
        return grad.astype(BF16).reshape(PLANES, part, channels)

    def by_owner(grad):
        return grad.reshape(groups, -1, channels)

    end_back, last_grads, *ffn_grads = tie(end_back, last_grads, *ffn_grads)
    ffn_grads.append(sum_line(last_grads))
    ends, by_core, *hidden = carry_axis(jnp.stack([end_back, total]), "c", F32, True, hidden)
    out_far, out_near = [feed_back(hidden, ffn_full, j, 2, CORES) for j in (1, 0)]
    ends, by_mid, out_far, d_branch = carry_axis(ends, "x", BF16, True, (out_far, d_branch))
    late, out_near, mixed_group = carry_planes(ends, (by_core, by_mid), True, (out_near, mixed_group))
    out_pair = (out_near.astype(F32) + swap(out_far, "c").astype(F32)).astype(BF16)
    out_side = scatter_side(out_pair) if mid == 2 else (scatter_side(out_pair),)
    d_conv, grad_inlet, grad_decay, core_sums = core_back(
        first, pulled, conv, sig_in, sig_dec, state, recur, coefs, carry, late, inlet_full, decay_full
    )
    branch_group = gather_group(d_branch)
    d_conv, branch_group = tie(d_conv, branch_group)
    behind = lax.ppermute(d_conv[:halo].astype(BF16), DP, [(j + 1, j) for j in range(groups - 1)])
    d_ext = jnp.concatenate([d_conv, behind.astype(F32)], axis=0)
    d_recur = vec_taps[0] * d_ext[:rows]
    for k in range(1, taps):
        d_recur = d_recur + vec_taps[k] * d_ext[k * seqs : k * seqs + rows]
    d_recur = d_recur.astype(BF16)
    recur_near = swap(d_recur, "x") if mid == 2 else lax.all_gather(d_recur, "x", axis=0, tiled=True)
    gates_b = fold_mid(fold_cores(jnp.concatenate([by_owner(grad_inlet), by_owner(grad_decay)], axis=1)))
    recur_near, dealt_other, *out_side = tie(recur_near, dealt_other, *out_side)
    mixed_sides = [lax.dynamic_index_in_dim(mixed_group.reshape(mid * CORES, 2, -1, channels), j, 1, keepdims=False)
                   .reshape(-1, channels) for j in (side, 1 - side)]
    grad_output = dot(dealt_own, mixed_sides[0]) + dot(dealt_other, mixed_sides[1])
    grad_branch = dot(normed_dealt, branch_group)
    packed = [by_plane(grad_output), by_plane(grad_branch), jnp.zeros((PLANES, part, channels), BF16), gates_b]
    recur_near, packed = tie(recur_near, jnp.concatenate(packed, axis=1))
    recur_near = jnp.concatenate([d_recur, recur_near], axis=0) if mid == 2 else recur_near
    grad_recur = by_plane(dot(normed_dealt, gather_rows(recur_near, "c")))
    packed = lax.dynamic_update_slice_in_dim(packed, grad_recur, 2 * part, 1)
    packed, d_recur, *ffn_grads = tie(packed, d_recur, *ffn_grads)
    sums = fold_planes(packed)
    d_normed = dot(d_branch, branch_full, ((1,), (1,))) + dot(d_recur, recur_full, ((1,), (1,)))
    dn_own, dn_other = halves(d_normed, "y")
    dn_got = swap(dn_other.astype(BF16), "y")
    dn_own = dn_own + dn_got.astype(F32)
    if mid == 2:
        out_side = [(out_side[0].astype(F32) + out_side[1].astype(F32)).astype(BF16)]
    out_side = out_side[0]
    scale_one = lax.rsqrt(jnp.mean(x_own * x_own, axis=-1, keepdims=True) + 1e-6)
    d_input, grad_gain_one = norm_back(x_own, scale_one, gain_one, dn_own)
    d_input = whole_rows((d_middle + d_input).astype(BF16), "y")

    shared = jnp.stack([grad_gain_one, jnp.sum(d_low_own.astype(F32), axis=0), grad_gain_two])
    shared = shared + swap(shared, "y")
    recur_sum = jnp.sum(d_recur.astype(F32), axis=0)
    by_unit = lax.dynamic_update_slice_in_dim(jnp.zeros((2, units), F32), jnp.concatenate(bias_grads, axis=1), my_start, 1)
    small = jnp.concatenate(
        [
            jnp.concatenate([branch_sum[:1], recur_sum[None], core_sums[4:], core_sums[3:4], core_sums[:3]], axis=0),
            shared.reshape(-1, channels),
            jnp.sum(d_out.astype(F32), axis=0).reshape(-1, channels),
            by_unit.reshape(-1, channels),
        ],
        axis=0,
    )
    small = sum_plane(small)
    returned = jnp.stack([grad.reshape(slices, part, 3 * step) for grad in ffn_grads], axis=1)
    small, returned = tie(small, returned)

    mask_own, _ = halves(mask, "y")
    result = jnp.where(mask_own, middle + scatter_rows(out_side, "x").astype(F32) + vec_shrink, 0.0).astype(BF16)
    result = whole_rows(result, "y")
    small = sum_planes(small)
    count = 6 + taps
    head_sums = lax.dynamic_slice_in_dim(small[:count].reshape(count, heads, head_size), place * head_part, head_part, 2)
    features = 4 * (width // channels)
    feature_sums = lax.dynamic_slice_in_dim(small[count : count + features].reshape(4, width), place * part, part, 1)
    unit_sums = small[count + features :].reshape(2, blocks, head_size)
    g_b_expand = lax.dynamic_slice_in_dim(unit_sums, place * head_part, head_part, 2)
    g_b_branch, g_b_recur, g_kernel = head_sums[0], head_sums[1], head_sums[2 : 2 + taps]
    g_conv_bias, g_b_inlet, g_b_decay, g_base = [head_sums[2 + taps + j] for j in range(4)]
    g_pre_gain, g_b_output, g_ffn_gain, g_b_shrink = [feature_sums[j] for j in range(4)]

    ffn_sum = to_slices(returned)
    grads_out = []
    for kind in range(3):
        pieces_out = []
        for j in range(slices):
            for k in range(chunks):
                keep = min(step, owned[j] * LANES - k * step)
                if keep > 0:
                    pieces_out.append(ffn_sum[j, k, :, kind * step : kind * step + keep])
        grads_out.append(jnp.concatenate(pieces_out, axis=1).astype(F32))
    grad_expand = jnp.stack(grads_out[:2])
    grad_shrink = grads_out[2]

    def gate_out(at):
        return sums[at : at + head_part].reshape(head_part, heads, head_size).transpose(1, 0, 2)

    def rows_out(v):
        return v.reshape(pieces, seqs, width).transpose(1, 0, 2)

    return (
        rows_out(result), rows_out(d_input), g_pre_gain, sums[part : 2 * part], g_b_branch, sums[2 * part : 3 * part], g_b_recur,
        g_kernel, g_conv_bias, gate_out(3 * part), g_b_inlet, gate_out(3 * part + head_part), g_b_decay, g_base,
        sums[:part], g_b_output, g_ffn_gain, grad_expand, g_b_expand, grad_shrink, g_b_shrink,
    )


def solution(mesh):
    groups, sides = mesh.shape["dp"], mesh.shape["tensor"]
    mid = groups // (PLANES * CORES)
    grid = Mesh(mesh.devices.reshape(PLANES, mid, CORES, sides), ("z", "x", "c", "y"))
    rows, vec = P(None, DP, None), P(DP)
    mat, head, tap, gate = P(DP, "y"), P("y", DP), P(None, "y", DP), P("y", DP, None)
    wide = P(None, DP, "y")
    return jax.shard_map(
        body,
        mesh=grid,
        in_specs=(
            rows, rows, P(), vec, mat, head, mat, head, tap, head, gate, head, gate, head, head, mat, vec, vec,
            wide, tap, mat, vec,
        ),
        out_specs=(
            rows, rows, vec, mat, head, mat, head, tap, head, gate, head, gate, head, head, mat, vec, vec,
            wide, tap, mat, vec,
        ),
        check_vma=False,
    )
```
